256 devices in a mesh: feat: 64 (over x, z, core), grp: 4 (over y).
Axes of the slice: x: 4, y: 4, z: 8, core: 2. Of those that a mesh axis runs over, the one named last changes fastest.
Arguments:
- features: bfloat16 [4, 4096, 8192], P('grp', 'feat'), may hold values from -6 to 6
- nbr_one: int32 [4, 10, 8192], P('grp'), may hold values from 0 to 8191
- w_one: bfloat16 [2, 4096, 512], P(None, 'feat'), may hold values from -0.09375 to 0.09375
- b_one: float32 [512], replicated, may hold values from -3 to 3
- send_rows: int32 [4, 64, 64, 4, 2], P('grp', 'feat'), may hold values from 0 to 127
- nbr_slot: int32 [4, 25, 8192], P('grp', None, 'feat'), may hold values from 0 to 511
- degree: int32 [4, 8192], P('grp', 'feat'), may hold values from 1 to 25
- w_two: bfloat16 [1024, 512], replicated, may hold values from -0.25 to 0.25
- cotangent: bfloat16 [4, 8192, 512], P('grp', 'feat'), may hold values from -6 to 6
Outputs:
- embedding: bfloat16 [4, 8192, 512], P('grp', 'feat')
- grad_w_one: float32 [2, 4096, 512], P(None, 'feat')
- grad_b_one: float32 [512], replicated
- grad_w_two: float32 [1024, 512], P(('feat', 'grp'))
The draws below stay inside these ranges and needn't reach their ends.
Inputs may be any that keep to these rules, and one draw needn't show every extreme that they name: `send_rows`: rows local to the owning device. Slots at or past degree are unused.
All inputs are finite; a program needn't handle non-finite values.
Results may differ from the reference program's by a relative error of at most 0.019.
The reference program's roundings to bfloat16 on the way count: a program that leaves them out, or rounds other values in their place, can miss the bound.
Values may be sent and summed in bfloat16 or wider, within the bound.
No kernel may reach another device: no remote copies, remote signals or barrier semaphores. Data moves between devices by JAX's collectives and lax.ppermute only.
A program may use at most 128 MiB of HBM per device.

```python
import jax
import jax.numpy as jnp
from jax import lax

F = 4096
H = 512
K_ONE = 10
K_TWO = 25
CAP = 2
NODE_DEV = 128
GROUPS = 4
FEATS = 64
PEERS = 256
NG = 8192


def touch_ends(values, key, least, largest):
    longest = values.shape.index(max(values.shape))
    spots = []
    for shift in (0, 1):
        where = [jax.random.randint(jax.random.fold_in(key, axis), (), 0, length) for axis, length in enumerate(values.shape)]
        where[longest] = (where[longest] + shift) % values.shape[longest]
        spots.append(tuple(where))
    return values.at[spots[0]].set(least).at[spots[1]].set(largest)


def block_levels(rng, extent, shards, smallest, high):
    loudness, own = 1.0, jax.random.fold_in(rng, 6)
    for position, shards_of in shards:
        steps = jnp.exp(jax.random.uniform(jax.random.fold_in(own, position), (shards_of,), jnp.float32, smallest / len(shards), high / len(shards)))
        loudness = loudness * jnp.repeat(steps, extent[position] // shards_of).reshape([-1 if axis == position else 1 for axis in range(len(extent))])
    return loudness


def bell_draw(stream_key, shape, width, bound, pieces=(), kind=jnp.bfloat16):
    result = width * jax.random.normal(stream_key, shape, jnp.float32)
    if pieces:
        result = result * block_levels(stream_key, shape, pieces, -0.22, 0.18)
    return jnp.clip(result, -bound, bound).astype(kind)


def setup_inputs(seed: int = 0) -> dict:
    splits = jax.random.split(jax.random.key(seed), 10)
    return {
        "features": bell_draw(splits[0], (GROUPS, F, NG), 1.0, 6.0, ((0, 4), (1, 64))),
        "nbr_one": touch_ends(jax.random.randint(splits[1], (GROUPS, K_ONE, NG), 0, NG), jax.random.fold_in(splits[1], 1), 0, NG - 1).astype(jnp.int32),
        "w_one": bell_draw(splits[2], (2, F, H), F ** -0.5, 0.09375, ((1, 64),)),
        "b_one": bell_draw(splits[3], (H,), 0.5, 3.0, (), jnp.float32),
        "send_rows": touch_ends(jax.random.randint(splits[4], (GROUPS, FEATS, FEATS, GROUPS, CAP), 0, NODE_DEV), jax.random.fold_in(splits[4], 1), 0, NODE_DEV - 1).astype(jnp.int32),
        "nbr_slot": touch_ends(jax.random.randint(splits[5], (GROUPS, K_TWO, NG), 0, PEERS * CAP), jax.random.fold_in(splits[5], 1), 0, (PEERS * CAP) - 1).astype(jnp.int32),
        "degree": touch_ends(jax.random.randint(splits[6], (GROUPS, NG), 1, K_TWO + 1), jax.random.fold_in(splits[6], 1), 1, K_TWO).astype(jnp.int32),
        "w_two": bell_draw(splits[7], (2 * H, H), H ** -0.5, 0.25),
        "cotangent": bell_draw(splits[8], (GROUPS, NG, H), 1.0, 6.0, ((0, 4), (1, 64))),
    }


def pick_columns(matrix, columns):
    return matrix[:, columns]


def reference(features, nbr_one, w_one, b_one, send_rows, nbr_slot, degree, w_two, cotangent):
    summed = jnp.zeros(features.shape, jnp.float32)
    for index in range(K_ONE):
        summed = summed + jax.vmap(pick_columns)(features, nbr_one[:, index, :]).astype(jnp.float32)
    agg_one = (summed / K_ONE).astype(jnp.bfloat16)

    def layer_one(pair):
        return (jnp.dot(pair[0].T, w_one[0], preferred_element_type=jnp.float32)
                + jnp.dot(pair[1].T, w_one[1], preferred_element_type=jnp.float32) + b_one)

    pre_one = lax.map(layer_one, (features, agg_one))
    h_one = jnp.maximum(pre_one, 0.0).astype(jnp.bfloat16)
    flat_h = h_one.reshape(GROUPS * NG, H)

    group_base = (jnp.arange(GROUPS, dtype=jnp.int32) * NG)[:, None, None, None, None]
    feat_base = (jnp.arange(FEATS, dtype=jnp.int32) * NODE_DEV)[None, :, None, None, None]
    global_rows = group_base + feat_base + send_rows
    by_requester = jnp.transpose(global_rows, (3, 2, 1, 0, 4)).reshape(GROUPS, FEATS, PEERS * CAP)
    owner_feat = (jnp.arange(NG, dtype=jnp.int32) // NODE_DEV).astype(jnp.int32)
    group_ids = jnp.arange(GROUPS, dtype=jnp.int32)
    rows_index = by_requester[group_ids[:, None, None], owner_feat[None, None, :], nbr_slot]
    live_mask = jnp.arange(K_TWO, dtype=jnp.int32)[None, :, None] < degree[:, None, :]
    degree_f = degree.astype(jnp.float32)

    accum = jnp.zeros((GROUPS, NG, H), jnp.float32)
    for index in range(K_TWO):
        picked = flat_h[rows_index[:, index, :]].astype(jnp.float32)
        accum = accum + jnp.where(live_mask[:, index, :, None], picked, 0.0)
    agg_two = (accum / degree_f[:, :, None]).astype(jnp.bfloat16)

    h_flat = h_one.reshape(-1, H)
    agg_flat = agg_two.reshape(-1, H)
    cot_flat = cotangent.reshape(-1, H)
    embedding = (jnp.dot(h_flat, w_two[:H], preferred_element_type=jnp.float32)
                 + jnp.dot(agg_flat, w_two[H:], preferred_element_type=jnp.float32)).astype(jnp.bfloat16)
    grad_w_two = jnp.concatenate([
        jnp.dot(h_flat.T, cot_flat, preferred_element_type=jnp.float32),
        jnp.dot(agg_flat.T, cot_flat, preferred_element_type=jnp.float32)], axis=0)

    d_self = jnp.dot(cot_flat, w_two[:H].T, preferred_element_type=jnp.float32)
    d_agg = jnp.dot(cot_flat, w_two[H:].T, preferred_element_type=jnp.float32)
    scaled = d_agg / degree_f.reshape(-1)[:, None]
    d_near = jnp.zeros((GROUPS * NG, H), jnp.float32)
    for index in range(K_TWO):
        live_now = live_mask[:, index, :].reshape(-1)[:, None]
        d_near = d_near.at[rows_index[:, index, :].reshape(-1)].add(jnp.where(live_now, scaled, 0.0))
    pre_flat = pre_one.reshape(-1, H)
    d_pre = jnp.where(pre_flat > 0.0, d_self + d_near, 0.0).astype(jnp.bfloat16)
    d_pre_groups = d_pre.reshape(GROUPS, NG, H)

    grad_self = jnp.zeros((F, H), jnp.float32)
    grad_near = jnp.zeros((F, H), jnp.float32)
    for group in range(GROUPS):
        grad_self = grad_self + jnp.dot(features[group], d_pre_groups[group], preferred_element_type=jnp.float32)
        grad_near = grad_near + jnp.dot(agg_one[group], d_pre_groups[group], preferred_element_type=jnp.float32)
    grad_w_one = jnp.stack([grad_self, grad_near], axis=0)
    grad_b_one = jnp.sum(d_pre.astype(jnp.float32), axis=0)
    return (embedding.reshape(GROUPS, NG, H), grad_w_one, grad_b_one, grad_w_two)
```

```python
import jax
import jax.numpy as jnp
from jax import lax
from jax.experimental import pallas as pl
from jax.experimental.pallas import tpu as pltpu
from jax.sharding import Mesh, PartitionSpec as P

BF = jnp.bfloat16
F32 = jnp.float32
NX, NZ, NC, NY = 4, 8, 2, 4
OFFS = (4, -3, 3, -2, 2, -1, 1, 0)
GROUPS_OF = ((0, 1), (2, 3), (4, 5), (6,), (7,))
FEAT = ("x", "z", "core")
ALL = ("x", "z", "core", "grp")
MIB = 1 << 20


def vmem():
    return pl.BlockSpec(memory_space=pltpu.VMEM)


def smem():
    return pl.BlockSpec(memory_space=pltpu.SMEM)


def call(body, outs, ins, args, name, scratch=(), limit=32):
    return pl.pallas_call(
        body,
        out_shape=outs,
        in_specs=ins,
        out_specs=jax.tree.map(lambda _: vmem(), outs),
        scratch_shapes=list(scratch),
        compiler_params=pltpu.CompilerParams(vmem_limit_bytes=limit * MIB),
        name=name,
    )(*args)


def shape(dims, kind):
    return jax.ShapeDtypeStruct(dims, kind)


def shift(value, axis, size, by):
    return lax.ppermute(value, axis, [(s, (s + by) % size) for s in range(size)])


def dot(a, b, ca, cb):
    return lax.dot_general(a, b, (((ca,), (cb,)), ((), ())), preferred_element_type=F32)


def mean_rows(fanout, idx, tbl, out, acc):
    nodes = acc.shape[0]

    def step(b, carry):
        for j in range(8):
            r = b * 8 + j
            rows = [tbl[idx[k * nodes + r]] for k in range(fanout)]
            while len(rows) > 1:
                rows = [
                    rows[i] + rows[i + 1] if i + 1 < len(rows) else rows[i]
                    for i in range(0, len(rows), 2)
                ]
            acc[pl.ds(r, 1), :] = rows[0]
        return carry

    lax.fori_loop(0, nodes // 8, step, 0)

    def finish(b, carry):
        s = pl.ds(pl.multiple_of(b * 128, 128), 128)
        out[s, :] = (acc[s, :] / float(fanout)).astype(BF)
        return carry

    lax.fori_loop(0, nodes // 128, finish, 0)


def gather_mean(idx, tbl, fanout):
    nodes = idx.shape[0] // fanout
    lanes = tbl.shape[-1]

    def body(*refs):
        mean_rows(fanout, *refs)

    return call(
        body, shape((nodes, lanes), BF), [smem(), vmem()], (idx, tbl), "neighbour_mean",
        [pltpu.VMEM((nodes, lanes), F32)], 40,
    )


def partial_pre(xs, aggs, ws):
    total = None
    for x_piece, a_piece, w in zip(xs, aggs, ws):
        term = dot(x_piece, w[0], 1, 0) + dot(a_piece, w[1], 1, 0)
        total = term if total is None else total + term
    return total


def block_kernel(n_blocks, has_recv, *refs):
    xs, aggs, ws = refs[:NX], refs[NX : 2 * NX], refs[2 * NX : 3 * NX]
    rest = refs[3 * NX :]
    for b in range(n_blocks):
        rows = pl.ds(b * 128, 128)
        total = partial_pre([x[b] for x in xs], [a[rows, :] for a in aggs], ws)
        if has_recv:
            total = total + rest[b][...]
            rest[n_blocks + b][...] = total
        else:
            rest[b][...] = total


def node_kernel(*refs):
    xs, aggs, ws = refs[:NX], refs[NX : 2 * NX], refs[2 * NX : 3 * NX]
    up, down, bias, d_self, returned, send, h_out, dpre_out, outgoing = refs[3 * NX :]
    pre = partial_pre([x[0] for x in xs], [a[...] for a in aggs], ws)
    pre = pre + (up[...] + down[...]) + bias[...]
    h = jnp.maximum(pre, 0.0).astype(BF)
    h_out[...] = h
    nodes = pre.shape[0]
    rows = lax.broadcasted_iota(jnp.int32, (nodes, send.shape[1]), 0)
    pick = (rows == send[...]).astype(F32).astype(BF)
    d_near = dot(pick, returned[...], 1, 0)
    dpre_out[...] = jnp.where(pre > 0.0, d_self[...] + d_near, 0.0).astype(BF)
    outgoing[...] = dot(pick, h, 0, 0).astype(BF)


def table_grad_kernel(cot, w_two, slot, deg_row, deg_col, d_table, d_self, counts):
    width = cot.shape[1]
    k_two = slot.shape[0]
    live = lax.broadcasted_iota(jnp.int32, slot.shape, 0) < deg_row[...]
    used = jnp.where(live, slot[...], -1)
    q = lax.broadcasted_iota(jnp.int32, counts.shape, 0)
    total = jnp.zeros(counts.shape, F32)
    for k in range(k_two):
        total = total + (q == used[k : k + 1, :]).astype(F32)
    ct = total.astype(BF)
    counts[...] = ct
    d_self[...] = dot(cot[...], w_two[:width, :], 1, 1)
    scaled = dot(cot[...], w_two[width:, :], 1, 1) / deg_col[...]
    hi = scaled.astype(BF)
    lo = (scaled - hi.astype(F32)).astype(BF)
    d_table[...] = (dot(ct, hi, 1, 0) + dot(ct, lo, 1, 0)).astype(BF)


def layer_two_kernel(meta, table, counts, deg_col, h, cot, w_two, emb, own, sib):
    width = cot.shape[1]
    agg = (dot(counts[...], table[...], 0, 0) / deg_col[...]).astype(BF)
    hv = h[...]
    emb[...] = (
        dot(hv, w_two[:width, :], 1, 0) + dot(agg, w_two[width:, :], 1, 0)
    ).astype(BF)
    first = meta[2] == 0
    half = own.shape[0] // 2
    for part, left in enumerate((hv, agg)):
        grad = dot(left, cot[...], 0, 0)
        grad = grad.reshape(half, 2, own.shape[1], width)
        rows = pl.ds(part * half, half)
        own[rows] = jnp.where(first, grad[:, 0], grad[:, 1])
        sib[rows] = jnp.where(first, grad[:, 1], grad[:, 0])


def two_core_sum_kernel(meta, own, recv, keep, out):
    for d in range(NX):
        chip = lax.rem(meta[0] + d, NX)
        total = own[chip] + recv[chip]
        if d == 0:
            keep[...] = total
        else:
            out[d - 1] = total.astype(BF)


def two_x_sum_kernel(own, r1, r2, r3, out):
    out[...] = (
        (own[...] + r2[...].astype(F32)) + (r1[...].astype(F32) + r3[...].astype(F32))
    ).astype(BF)


def rows_total(pieces):
    evens = (pieces[0] + pieces[4]) + (pieces[2] + pieces[6])
    odds = (pieces[1] + pieces[5]) + (pieces[3] + pieces[7])
    return evens + odds


def weight_grad_kernel(n_pieces, *refs):
    xs = refs[:NX]
    aggs = refs[NX : NX + NX * n_pieces]
    dps = refs[NX + NX * n_pieces : NX + NX * n_pieces + NZ]
    own, sib, dp = refs[-3:]
    half = own.shape[1] // 2 - 8
    by_offset = {}
    for b in range(NZ):
        v = dps[b][...]
        dp[pl.ds(b * 128, 128), :] = v
        by_offset[OFFS[b] % NZ] = jnp.sum(v.astype(F32), axis=0, keepdims=True)
    bias = rows_total([by_offset[o] for o in range(NZ)])
    d_all = dp[...]
    for d in range(NX):
        x_all = xs[d][...].reshape(d_all.shape[0], -1)
        a_all = jnp.concatenate([a[...] for a in aggs[d * n_pieces : (d + 1) * n_pieces]], axis=0)
        for part, left in enumerate((x_all, a_all)):
            grad = dot(left, d_all, 0, 0)
            own[d, pl.ds(part * half, half), :] = grad[:half]
            sib[d, pl.ds(part * half, half), :] = grad[half:]
        tail = jnp.broadcast_to(bias, (16, bias.shape[1]))
        own[d, pl.ds(2 * half, 16), :] = tail
        sib[d, pl.ds(2 * half, 16), :] = tail


def one_core_sum_kernel(own, recv, p0, p1, p2, p3):
    for d, out in enumerate((p0, p1, p2, p3)):
        out[...] = (own[d] + recv[d]).astype(BF)


def four_sum(parts):
    p0, p1, p2, p3 = [p[...].astype(F32) for p in parts]
    return (p0 + p2) + (p1 + p3)


def one_x_sum_kernel(p0, p1, p2, p3, out):
    out[...] = four_sum((p0, p1, p2, p3)).astype(BF)


def one_y_sum_kernel(p0, p1, p2, p3, grad, bias):
    total = four_sum((p0, p1, p2, p3))
    half = grad.shape[1]
    grad[0] = total[:half]
    grad[1] = total[half : 2 * half]
    bias[...] = total[2 * half : 2 * half + 1]


def on_device(features, nbr_one, w_one, b_one, send_rows, nbr_slot, degree, w_two, cotangent):
    local = features[0]
    feats, group_nodes = local.shape
    fanout = nbr_one.shape[1]
    width = w_two.shape[1]
    owned = cotangent.shape[1]
    x_at, z_at = lax.axis_index("x"), lax.axis_index("z")
    core, grp = lax.axis_index("core"), lax.axis_index("grp")
    meta = jnp.stack([x_at, z_at, core, grp]).astype(jnp.int32)
    swap = lambda v: shift(v, "core", NC, 1)

    deg = degree[0]
    deg_col = deg.astype(F32)[:, None]
    cot = cotangent[0]
    slots = NX * NZ * NC * NY * send_rows.shape[-1]
    d_table, d_self, counts = call(
        table_grad_kernel,
        (shape((slots, width), BF), shape((owned, width), F32), shape((slots, owned), BF)),
        [vmem()] * 5,
        (cot, w_two, nbr_slot[0], deg[None, :], deg_col),
        "table_grad",
    )

    def exchange(rows):
        moved = lax.all_to_all(
            rows.reshape(NX * NZ * NC * NY, -1, width), ALL, split_axis=0, concat_axis=0, tiled=True
        )
        return moved.reshape(-1, width)

    returned = exchange(d_table)

    sibling = swap(local)
    both = jnp.concatenate([local, sibling], axis=0)
    node_major = both.T
    tbl = node_major.astype(F32)[:, None, :]
    z_order = (z_at + jnp.array([o % NZ for o in OFFS], jnp.int32)) % NZ
    x_order = (x_at + jnp.arange(NX, dtype=jnp.int32)) % NX
    blocks = ((x_order[None, :] * NZ + z_order[:, None]) * NC + core).reshape(-1)
    idx_all = jnp.take(
        nbr_one[0].reshape(fanout, -1, owned), blocks, axis=1
    )
    idx_all = idx_all.reshape(fanout, NZ, NX, owned)
    x_blocks = jnp.take(
        node_major.reshape(-1, owned, NC * feats),
        ((x_order[:, None] * NZ + z_order[None, :]) * NC + core).reshape(-1),
        axis=0,
    ).reshape(NX, NZ, owned, NC * feats)
    xs = [x_blocks[0]] + [shift(x_blocks[d], "x", NX, d) for d in range(1, NX)]
    w_pair = jnp.concatenate([w_one, swap(w_one)], axis=1)
    ws = [w_pair] + [shift(w_pair, "x", NX, d) for d in range(1, NX)]

    pieces = [[] for _ in range(NX)]
    received = {}
    token = None
    for group in GROUPS_OF:
        n = len(group)
        idx = idx_all[:, group[0] : group[0] + n].transpose(0, 2, 1, 3).reshape(-1)
        agg = gather_mean(idx, tbl, fanout).reshape(NX, n * owned, NC * feats)
        mine = [agg[0]] + [shift(agg[d], "x", NX, d) for d in range(1, NX)]
        for d in range(NX):
            pieces[d].append(mine[d])
        x_part = [x[group[0] : group[0] + n] for x in xs]
        if group[0] == len(OFFS) - 1:
            break
        recv = [received[OFFS[b]] for b in group] if group[0] >= 2 else []
        partial = call(
            lambda *refs, n=n, r=bool(recv): block_kernel(n, r, *refs),
            tuple(shape((owned, width), F32) for _ in range(n)),
            [vmem()] * (3 * NX + len(recv)),
            (*x_part, *mine, *ws, *recv),
            "block_pre",
        )
        for b, value in zip(group, partial):
            off = OFFS[b]
            step = 1 if off > 0 else -1
            received[off - step if off - step else ("up" if step > 0 else "down")] = shift(
                value, "z", NZ, step
            )

    send = send_rows[0, 0].reshape(1, -1)
    h_one, d_pre, outgoing = call(
        node_kernel,
        (shape((owned, width), BF), shape((owned, width), BF), shape((slots, width), BF)),
        [vmem()] * (3 * NX + 6),
        (
            *x_part, *mine, *ws, received["up"], received["down"], b_one[None, :], d_self,
            returned, send,
        ),
        "node_update",
    )

    d_pre_at = {0: d_pre}
    for step, last in ((-1, 4), (1, 3)):
        value = d_pre
        for o in range(1, last + 1):
            value = shift(value, "z", NZ, step)
            d_pre_at[-step * o] = value
    table = exchange(outgoing)

    block_rows = 2 * width // (NX * NZ * NC)
    emb, two_own, two_sib = call(
        layer_two_kernel,
        (
            shape((owned, width), BF),
            shape((NX * NZ, block_rows, width), F32),
            shape((NX * NZ, block_rows, width), F32),
        ),
        [smem()] + [vmem()] * 6,
        (meta, table, counts, deg_col, h_one, cot, w_two),
        "layer_two",
    )
    two_recv = swap(two_sib)
    per_chip = NZ * block_rows
    keep, sent = call(
        two_core_sum_kernel,
        (shape((per_chip, width), F32), shape((NX - 1, per_chip, width), BF)),
        [smem(), vmem(), vmem()],
        (meta, two_own.reshape(NX, per_chip, width), two_recv.reshape(NX, per_chip, width)),
        "two_core_sum",
    )
    two_got = [shift(sent[d - 1], "x", NX, d) for d in range(1, NX)]
    two_x = call(
        two_x_sum_kernel, shape((per_chip, width), BF), [vmem()] * NX, (keep, *two_got), "two_x_sum"
    )
    two_last = lax.all_to_all(
        two_x.reshape(NZ * NY, -1, width), ("z", "grp"), split_axis=0, concat_axis=0, tiled=True
    )
    grad_w_two = jnp.sum(two_last.astype(F32), axis=0)

    rows = 2 * feats + 16
    n_pieces = len(GROUPS_OF)
    one_own, one_sib = call(
        lambda *refs: weight_grad_kernel(n_pieces, *refs),
        (shape((NX, rows, width), F32), shape((NX, rows, width), F32)),
        [vmem()] * (NX + NX * n_pieces + NZ),
        (*xs, *[p for d in range(NX) for p in pieces[d]], *[d_pre_at[o] for o in OFFS]),
        "weight_grad",
        [pltpu.VMEM((NZ * owned, width), BF)],
    )
    one_recv = swap(one_sib)
    parts = call(
        one_core_sum_kernel,
        tuple(shape((rows, width), BF) for _ in range(NX)),
        [vmem()] * 2,
        (one_own, one_recv),
        "one_core_sum",
    )
    got = [parts[0]] + [shift(parts[d], "x", NX, -d) for d in range(1, NX)]
    one_x = call(one_x_sum_kernel, shape((rows, width), BF), [vmem()] * NX, tuple(got), "one_x_sum")
    got = [one_x] + [shift(one_x, "grp", NY, d) for d in range(1, NY)]
    grad_w_one, grad_b_one = call(
        one_y_sum_kernel,
        (shape((2, feats, width), F32), shape((1, width), F32)),
        [vmem()] * NY,
        tuple(got),
        "one_y_sum",
    )
    return emb[None], grad_w_one, grad_b_one[0], grad_w_two


def solution(mesh):
    parts = Mesh(mesh.devices.reshape(NX, NZ, NC, NY), ALL)
    return jax.shard_map(
        on_device,
        mesh=parts,
        in_specs=(
            P("grp", FEAT, None),
            P("grp", None, None),
            P(None, FEAT, None),
            P(),
            P("grp", FEAT, None, None, None),
            P("grp", None, FEAT),
            P("grp", FEAT),
            P(),
            P("grp", FEAT, None),
        ),
        out_specs=(P("grp", FEAT, None), P(None, FEAT, None), P(), P(ALL, None)),
        check_vma=False,
    )
```

```python
import jax
import jax.numpy as jnp
from jax import lax
from jax.experimental import pallas as pl
from jax.experimental.pallas import tpu as pltpu
from jax.sharding import Mesh, PartitionSpec as P

BF = jnp.bfloat16
F32 = jnp.float32
NX, NZ, NC, NY = 4, 8, 2, 4
CHIPS = NX * NZ
STEPS = 4
MEAN_STEPS = 8
FIRST_MEANS = 3
FEAT = ("x", "z", "core")
CHIP = ("x", "z")
ALL = ("x", "z", "core", "grp")
LIMIT = 60 << 20


def vmem():
    return pl.BlockSpec()


def unread():
    return pl.BlockSpec(memory_space=pl.ANY)


def smem():
    return pl.BlockSpec(memory_space=pltpu.SMEM)


def call(body, outs, ins, args, name, scratch=(), us=1.0, grid=None, out_specs=None, alias=None):
    extra = {} if grid is None else {"grid": grid}
    if alias:
        extra["input_output_aliases"] = alias
    return pl.pallas_call(
        body,
        out_shape=outs,
        in_specs=ins,
        out_specs=jax.tree.map(lambda _: vmem(), outs) if out_specs is None else out_specs,
        scratch_shapes=list(scratch),
        cost_estimate=pl.CostEstimate(flops=0, bytes_accessed=int(us * 3.6e6), transcendentals=0),
        compiler_params=pltpu.CompilerParams(vmem_limit_bytes=LIMIT),
        name=name,
        **extra,
    )(*args)


def whole(dims):
    return pl.BlockSpec(dims, lambda i: (0,) * len(dims))


def shape(dims, kind):
    return jax.ShapeDtypeStruct(dims, kind)


def shift(value, axis, size, by):
    return lax.ppermute(value, axis, [(s, (s + by) % size) for s in range(size)])


def dot(a, b, ca, cb):
    return lax.dot_general(a, b, (((ca,), (cb,)), ((), ())), preferred_element_type=F32)


def table_kernel(owned, meta, own, sib, tbl):
    core = meta[0]
    first = core == 0
    def step(chip, carry):
        for c in range(NC):
            cols = pl.ds(pl.multiple_of((chip * NC + c) * owned, owned), owned)
            a, b = own[:, cols].astype(F32), sib[:, cols].astype(F32)
            pair = jnp.concatenate([jnp.where(first, a, b), jnp.where(first, b, a)], axis=0)
            tbl[cols, :] = pair.T
        return carry

    lax.fori_loop(0, CHIPS, step, 0, unroll=2)


def own_rows(core, tbl, mine):
    owned = mine.shape[1]

    def copy(chip, carry):
        at = pl.multiple_of((chip * NC + core) * owned, owned)
        mine[chip] = tbl[pl.ds(at, owned), :].astype(BF)
        return carry

    lax.fori_loop(0, CHIPS, copy, 0)


def mean_rows(fanout, first, idx, tbl, out, acc):
    owned = acc.shape[0]
    per = out.shape[0]

    def chunk(c, carry):
        base = ((first + pl.program_id(0)) * per + c) * (fanout * owned)

        def step(b, inner):
            for j in range(16):
                r = b * 16 + j
                rows = [tbl[pl.ds(idx[base + k * owned + r], 1), :] for k in range(fanout)]
                while len(rows) > 1:
                    rows = [
                        rows[i] + rows[i + 1] if i + 1 < len(rows) else rows[i]
                        for i in range(0, len(rows), 2)
                    ]
                acc[pl.ds(r, 1), :] = rows[0]
            return inner

        lax.fori_loop(0, owned // 16, step, 0)
        out[c] = (acc[...] / float(fanout)).astype(BF)
        return carry

    lax.fori_loop(0, per, chunk, 0)


def first_mean_kernel(fanout, meta, idx, tbl, after, out, mine, acc):
    @pl.when(pl.program_id(0) == 0)
    def _():
        own_rows(meta[0], tbl, mine)

    mean_rows(fanout, 0, idx, tbl, out, acc)


def last_mean_kernel(fanout, idx, tbl, begun, after, out, acc):
    mean_rows(fanout, FIRST_MEANS, idx, tbl, out, acc)


def by_row(deg_row, width):
    n = deg_row.shape[1]
    square = jnp.broadcast_to(deg_row[...].astype(F32), (n, n)).T
    return jnp.concatenate([square] * (width // n), axis=1)


def add_product(left, w, acc):
    per = left.shape[0]
    feats = w.shape[2]
    rows = w[...].reshape(per * NC * feats, w.shape[3])
    lhs = jnp.concatenate([left[i] for i in range(per)], axis=1)
    term = dot(lhs, rows, 1, 0)

    @pl.when(pl.program_id(0) == 0)
    def _():
        acc[...] = term

    @pl.when(pl.program_id(0) > 0)
    def _():
        acc[...] += term


def self_kernel(left, w, out):
    add_product(left, w, out)


def node_kernel(
    left, w, self_part, bias, d_self, returned, send, h_out, dpre_out, outgoing, acc
):
    add_product(left, w, acc)

    @pl.when(pl.program_id(0) == STEPS - 1)
    def _():
        pre = self_part[...] + acc[...] + bias[...]
        h = jnp.maximum(pre, 0.0).astype(BF)
        h_out[...] = h
        rows = lax.broadcasted_iota(jnp.int32, (pre.shape[0], send.shape[1]), 0)
        pick = (rows == send[...]).astype(F32).astype(BF)
        d_near = dot(pick, returned[...], 1, 0)
        dpre_out[...] = jnp.where(pre > 0.0, d_self[...] + d_near, 0.0).astype(BF)
        outgoing[...] = dot(pick, h, 0, 0).astype(BF)


def table_grad_kernel(cot, w_two, slot, deg_row, d_table, d_self, counts):
    width = cot.shape[1]
    k_two = slot.shape[1]
    live = lax.broadcasted_iota(jnp.int32, slot.shape[1:], 0) < deg_row[...]
    used = jnp.where(live, slot[0], -1)
    q = lax.broadcasted_iota(jnp.int32, counts.shape, 0)
    total = jnp.zeros(counts.shape, F32)
    for k in range(k_two):
        total = total + (q == used[k : k + 1, :]).astype(F32)
    ct = total.astype(BF)
    counts[...] = ct
    d_self[...] = dot(cot[...], w_two[:width, :], 1, 1)
    scaled = dot(cot[...], w_two[width:, :], 1, 1) / by_row(deg_row, width)
    hi = scaled.astype(BF)
    lo = (scaled - hi.astype(F32)).astype(BF)
    d_table[...] = (dot(ct, hi, 1, 0) + dot(ct, lo, 1, 0)).astype(BF)


def layer_two_kernel(meta, table, counts, deg_row, h, cot, w_two, emb, own, sib):
    width = cot.shape[1]
    agg = (dot(counts[...], table[...], 0, 0) / by_row(deg_row, width)).astype(BF)
    hv = h[...]
    emb[...] = (
        dot(hv, w_two[:width, :], 1, 0) + dot(agg, w_two[width:, :], 1, 0)
    ).astype(BF)
    first = meta[0] == 0
    half = own.shape[0] // 2
    for part, left in enumerate((hv, agg)):
        grad = dot(left, cot[...], 0, 0)
        grad = grad.reshape(half, 2, own.shape[1], width)
        rows = pl.ds(part * half, half)
        own[rows] = jnp.where(first, grad[:, 0], grad[:, 1])
        sib[rows] = jnp.where(first, grad[:, 1], grad[:, 0]).astype(BF)


def weight_grad_kernel(meta, left, d_pre, own, sib):
    lanes = left.shape[2]
    nodes = left.shape[1] // 2
    half = lanes // 2
    first = meta[0] == 0
    d_all = d_pre[...]
    for part in range(2):
        grad = dot(left[0, pl.ds(part * nodes, nodes), :], d_all, 0, 0)
        rows = pl.ds(part * half, half)
        own[0, rows, :] = jnp.where(first, grad[:half], grad[half:])
        sib[0, rows, :] = jnp.where(first, grad[half:], grad[:half])
    bias = jnp.sum(d_all.astype(F32), axis=0, keepdims=True)
    tail = jnp.broadcast_to(bias, (16, bias.shape[1]))
    own[0, pl.ds(lanes, 16), :] = tail
    sib[0, pl.ds(lanes, 16), :] = tail


def core_sum_kernel(one_own, one_recv, two_own, two_recv, out):
    rows = one_own.shape[1]
    out[:, :rows, :] = (one_own[...] + one_recv[...]).astype(BF)
    out[:, rows:, :] = (two_own[...] + two_recv[...].astype(F32)).astype(BF)


def sum_first(ref):
    total = ref[0].astype(F32)
    for i in range(1, ref.shape[0]):
        total = total + ref[i].astype(F32)
    return total


def x_sum_kernel(parts, out):
    total = sum_first(parts).astype(BF)
    n = parts.shape[1] - out.shape[1]
    two = n * NY // (NY - 1)
    one = parts.shape[1] - two
    each = two // NY
    per = each // NZ
    to = lax.broadcasted_iota(jnp.int32, (two, two), 0)
    at = lax.broadcasted_iota(jnp.int32, (two, two), 1)
    source = (lax.rem(lax.div(to, per), NZ) * NY + lax.div(to, each)) * per + lax.rem(to, per)
    order = (at == source).astype(F32).astype(BF)
    moved = dot(order, total[one:], 1, 0).astype(BF)
    for y in range(NY):
        out[y, :one, :] = total[:one]
        out[y, one:, :] = moved[y * each : (y + 1) * each]


def y_sum_kernel(parts, grad, bias, two):
    total = sum_first(parts)
    half = grad.shape[1]
    grad[0] = total[:half]
    grad[1] = total[half : 2 * half]
    bias[...] = total[2 * half : 2 * half + 1]
    two[...] = total[2 * half + 16 :]


def all_to_all(value, axes):
    return lax.all_to_all(value, axes, split_axis=0, concat_axis=0, tiled=True)


def on_device(features, nbr_one, w_one, b_one, send_rows, nbr_slot, degree, w_two, cotangent):
    local = features[0]
    feats, group_nodes = local.shape
    fanout = nbr_one.shape[1]
    width = w_two.shape[1]
    owned = cotangent.shape[1]
    lanes = NC * feats
    per = CHIPS // STEPS
    core = lax.axis_index("core")
    meta = jnp.full((1,), core, jnp.int32)
    swap = lambda v: shift(v, "core", NC, 1)

    sibling = swap(local)
    w_all = lax.all_gather(w_one.reshape(-1, width), FEAT, axis=0, tiled=True)
    w_all = w_all.reshape(CHIPS * NC, 2, feats, width)

    deg_row = degree[0][None, :]
    cot = cotangent[0]
    slots = CHIPS * NC * NY * send_rows.shape[-1]
    d_table, d_self, counts = call(
        table_grad_kernel,
        (shape((slots, width), BF), shape((owned, width), F32), shape((slots, owned), BF)),
        [vmem()] * 4,
        (cot, w_two, nbr_slot, deg_row),
        "table_grad", us=3.0,
    )

    def exchange(rows):
        return all_to_all(rows.reshape(CHIPS * NC * NY, -1, width), ALL).reshape(-1, width)

    returned = exchange(d_table)

    tbl = call(
        lambda *refs: table_kernel(owned, *refs),
        shape((group_nodes, lanes), F32),
        [smem(), vmem(), vmem()],
        (meta, local, sibling),
        "node_table", us=6.0,
    )
    by_device = nbr_one[0].reshape(fanout, CHIPS, NC, owned)
    idx = lax.dynamic_index_in_dim(by_device, core, 2, keepdims=False)
    idx = idx.transpose(1, 0, 2).reshape(-1)
    mean_shape = shape((CHIPS, owned, lanes), BF)
    mean_per = CHIPS // MEAN_STEPS
    acc = [pltpu.VMEM((owned, lanes), F32)]
    us_per = idx.shape[0] * 1e-3 / MEAN_STEPS
    begun, mine = call(
        lambda *refs: first_mean_kernel(fanout, *refs),
        (mean_shape, mean_shape),
        [smem(), smem(), whole(tbl.shape), unread()],
        (meta, idx, tbl, d_table),
        "mean_first", acc, us_per * FIRST_MEANS, (FIRST_MEANS,),
        (pl.BlockSpec((mean_per, owned, lanes), lambda i: (i, 0, 0)), whole(mean_shape.shape)),
    )
    feats_here = all_to_all(mine, CHIP)
    last = MEAN_STEPS - FIRST_MEANS
    means = call(
        lambda *refs: last_mean_kernel(fanout, *refs),
        mean_shape,
        [smem(), whole(tbl.shape), unread(), unread()],
        (idx, tbl, begun, returned),
        "mean_last", acc, us_per * last, (last,),
        pl.BlockSpec((mean_per, owned, lanes), lambda i: (i + FIRST_MEANS, 0, 0)),
        {2: 0},
    )
    means_here = all_to_all(means, CHIP)

    left_spec = pl.BlockSpec((per, owned, lanes), lambda i: (i, 0, 0))

    def w_spec(part):
        return pl.BlockSpec((per * NC, 1, feats, width), lambda i: (i, part, 0, 0))

    self_part = call(
        self_kernel, shape((owned, width), F32), [left_spec, w_spec(0)], (feats_here, w_all),
        "self_part", us=4.0, grid=(STEPS,), out_specs=whole((owned, width)),
    )
    send = send_rows[0, 0].reshape(1, -1)
    bias_row = b_one[None, :]
    ins = (self_part, bias_row, d_self, returned, send)
    outs = (shape((owned, width), BF), shape((owned, width), BF), shape((slots, width), BF))
    h_one, d_pre, outgoing = call(
        node_kernel,
        outs,
        [left_spec, w_spec(1)] + [whole(v.shape) for v in ins],
        (means_here, w_all, *ins),
        "node_update",
        [pltpu.VMEM((owned, width), F32)],
        us=4.0, grid=(STEPS,), out_specs=tuple(whole(o.shape) for o in outs),
    )
    d_pre_z = lax.all_gather(d_pre, "z", axis=0, tiled=True)
    both = jnp.concatenate(
        [mine.reshape(NX, NZ * owned, lanes), means.reshape(NX, NZ * owned, lanes)], axis=1
    )
    both, table = lax.optimization_barrier((both, exchange(outgoing)))
    left = all_to_all(both, "x")

    block_rows = 2 * width // (CHIPS * NC)
    emb, two_own, two_sib = call(
        layer_two_kernel,
        (
            shape((owned, width), BF),
            shape((CHIPS, block_rows, width), F32),
            shape((CHIPS, block_rows, width), BF),
        ),
        [smem()] + [vmem()] * 6,
        (meta, table, counts, deg_row, h_one, cot, w_two),
        "layer_two", us=3.0,
    )
    d_pre_z, two_sib = lax.optimization_barrier((d_pre_z, two_sib))
    two_recv = swap(two_sib)

    rows = 2 * feats + 16
    one_spec = pl.BlockSpec((1, rows, width), lambda i: (i, 0, 0))
    one_own, one_sib = call(
        weight_grad_kernel,
        (shape((NX, rows, width), F32), shape((NX, rows, width), F32)),
        [
            smem(), pl.BlockSpec((1, 2 * NZ * owned, lanes), lambda i: (i, 0, 0)),
            whole(d_pre_z.shape),
        ],
        (meta, left, d_pre_z),
        "weight_grad",
        us=4.0, grid=(NX,), out_specs=(one_spec, one_spec),
    )
    one_recv = swap(one_sib)
    two_rows = NZ * block_rows
    sums = call(
        core_sum_kernel,
        shape((NX, rows + two_rows, width), BF),
        [vmem()] * 4,
        (
            one_own, one_recv, two_own.reshape(NX, two_rows, width),
            two_recv.reshape(NX, two_rows, width),
        ),
        "core_sum",
    )
    sums = call(
        x_sum_kernel, shape((NY, rows + two_rows // NY, width), BF), [vmem()],
        (all_to_all(sums, "x"),), "x_sum",
    )
    grad_w_one, grad_b_one, two = call(
        y_sum_kernel,
        (
            shape((2, feats, width), F32), shape((1, width), F32),
            shape((two_rows // NY, width), F32),
        ),
        [vmem()],
        (all_to_all(sums, "grp"),),
        "y_sum",
    )
    grad_w_two = jnp.sum(all_to_all(two.reshape(NZ, -1, width), "z"), axis=0)
    return emb[None], grad_w_one, grad_b_one[0], grad_w_two


def solution(mesh):
    parts = Mesh(mesh.devices.reshape(NX, NZ, NC, NY), ALL)
    return jax.shard_map(
        on_device,
        mesh=parts,
        in_specs=(
            P("grp", FEAT, None),
            P("grp", None, None),
            P(None, FEAT, None),
            P(),
            P("grp", FEAT, None, None, None),
            P("grp", None, FEAT),
            P("grp", FEAT),
            P(),
            P("grp", FEAT, None),
        ),
        out_specs=(P("grp", FEAT, None), P(None, FEAT, None), P(), P(ALL, None)),
        check_vma=False,
    )
```

```python
import jax
import jax.numpy as jnp
from jax import lax
from jax.experimental import pallas as pl
from jax.experimental.pallas import tpu as pltpu
from jax.sharding import Mesh, PartitionSpec as P

BF = jnp.bfloat16
F32 = jnp.float32
NX, NZ, NC, NY = 4, 8, 2, 4
CHIPS = NX * NZ
STEPS = 4
MEAN_STEPS = 8
FIRST_MEANS = 2
FEAT = ("x", "z", "core")
CHIP = ("x", "z")
ALL = ("x", "z", "core", "grp")
LIMIT = 60 << 20


def vmem():
    return pl.BlockSpec()


def unread():
    return pl.BlockSpec(memory_space=pl.ANY)


def smem():
    return pl.BlockSpec(memory_space=pltpu.SMEM)


def call(body, outs, ins, args, name, scratch=(), us=1.0, grid=None, out_specs=None, alias=None):
    extra = {} if grid is None else {"grid": grid}
    if alias:
        extra["input_output_aliases"] = alias
    return pl.pallas_call(
        body,
        out_shape=outs,
        in_specs=ins,
        out_specs=jax.tree.map(lambda _: vmem(), outs) if out_specs is None else out_specs,
        scratch_shapes=list(scratch),
        cost_estimate=pl.CostEstimate(flops=0, bytes_accessed=int(us * 3.6e6), transcendentals=0),
        compiler_params=pltpu.CompilerParams(vmem_limit_bytes=LIMIT),
        name=name,
        **extra,
    )(*args)


def whole(dims):
    return pl.BlockSpec(dims, lambda i: (0,) * len(dims))


def shape(dims, kind):
    return jax.ShapeDtypeStruct(dims, kind)


def shift(value, axis, size, by):
    return lax.ppermute(value, axis, [(s, (s + by) % size) for s in range(size)])


def dot(a, b, ca, cb):
    return lax.dot_general(a, b, (((ca,), (cb,)), ((), ())), preferred_element_type=F32)


def table_kernel(owned, meta, own, sib, tbl):
    core = meta[0]
    first = core == 0
    def step(chip, carry):
        for c in range(NC):
            cols = pl.ds(pl.multiple_of((chip * NC + c) * owned, owned), owned)
            a, b = own[:, cols].astype(F32), sib[:, cols].astype(F32)
            pair = jnp.concatenate([jnp.where(first, a, b), jnp.where(first, b, a)], axis=0)
            tbl[cols, :] = pair.T
        return carry

    lax.fori_loop(0, CHIPS, step, 0, unroll=2)


def own_rows(core, tbl, mine):
    owned = mine.shape[1]

    def copy(chip, carry):
        at = pl.multiple_of((chip * NC + core) * owned, owned)
        mine[chip] = tbl[pl.ds(at, owned), :].astype(BF)
        return carry

    lax.fori_loop(0, CHIPS, copy, 0)


def mean_rows(fanout, first, idx, tbl, out, acc):
    owned = acc.shape[0]
    per = out.shape[0]

    def chunk(c, carry):
        base = ((first + pl.program_id(0)) * per + c) * (fanout * owned)

        def step(b, inner):
            for j in range(16):
                r = b * 16 + j
                rows = [tbl[pl.ds(idx[base + k * owned + r], 1), :] for k in range(fanout)]
                while len(rows) > 1:
                    rows = [
                        rows[i] + rows[i + 1] if i + 1 < len(rows) else rows[i]
                        for i in range(0, len(rows), 2)
                    ]
                acc[pl.ds(r, 1), :] = rows[0]
            return inner

        lax.fori_loop(0, owned // 16, step, 0)
        out[c] = (acc[...] / float(fanout)).astype(BF)
        return carry

    lax.fori_loop(0, per, chunk, 0)


def first_mean_kernel(fanout, meta, idx, tbl, after, out, mine, acc):
    @pl.when(pl.program_id(0) == 0)
    def _():
        own_rows(meta[0], tbl, mine)

    mean_rows(fanout, 0, idx, tbl, out, acc)


def last_mean_kernel(fanout, idx, tbl, begun, after, out, acc):
    mean_rows(fanout, FIRST_MEANS, idx, tbl, out, acc)


def by_row(deg_row, width):
    n = deg_row.shape[1]
    square = jnp.broadcast_to(deg_row[...].astype(F32), (n, n)).T
    return jnp.concatenate([square] * (width // n), axis=1)


def add_product(left, w, acc):
    per = left.shape[0]
    feats = w.shape[2]
    rows = w[...].reshape(per * NC * feats, w.shape[3])
    lhs = jnp.concatenate([left[i] for i in range(per)], axis=1)
    term = dot(lhs, rows, 1, 0)

    @pl.when(pl.program_id(0) == 0)
    def _():
        acc[...] = term

    @pl.when(pl.program_id(0) > 0)
    def _():
        acc[...] += term


def self_kernel(left, w, out):
    add_product(left, w, out)


def node_kernel(
    left, w, self_part, bias, d_self, returned, send, h_out, dpre_out, outgoing, acc
):
    add_product(left, w, acc)

    @pl.when(pl.program_id(0) == STEPS - 1)
    def _():
        pre = self_part[...] + acc[...] + bias[...]
        h = jnp.maximum(pre, 0.0).astype(BF)
        h_out[...] = h
        rows = lax.broadcasted_iota(jnp.int32, (pre.shape[0], send.shape[1]), 0)
        pick = (rows == send[...]).astype(F32).astype(BF)
        d_near = dot(pick, returned[...], 1, 0)
        dpre_out[...] = jnp.where(pre > 0.0, d_self[...] + d_near, 0.0).astype(BF)
        outgoing[...] = dot(pick, h, 0, 0).astype(BF)


def table_grad_kernel(cot, w_two, slot, deg_row, d_table, d_self, counts):
    width = cot.shape[1]
    k_two = slot.shape[1]
    live = lax.broadcasted_iota(jnp.int32, slot.shape[1:], 0) < deg_row[...]
    used = jnp.where(live, slot[0], -1)
    q = lax.broadcasted_iota(jnp.int32, counts.shape, 0)
    total = jnp.zeros(counts.shape, F32)
    for k in range(k_two):
        total = total + (q == used[k : k + 1, :]).astype(F32)
    ct = total.astype(BF)
    counts[...] = ct
    d_self[...] = dot(cot[...], w_two[:width, :], 1, 1)
    scaled = dot(cot[...], w_two[width:, :], 1, 1) / by_row(deg_row, width)
    hi = scaled.astype(BF)
    lo = (scaled - hi.astype(F32)).astype(BF)
    d_table[...] = (dot(ct, hi, 1, 0) + dot(ct, lo, 1, 0)).astype(BF)


def layer_two_kernel(meta, table, counts, deg_row, h, cot, w_two, emb, own, sib):
    width = cot.shape[1]
    agg = (dot(counts[...], table[...], 0, 0) / by_row(deg_row, width)).astype(BF)
    hv = h[...]
    emb[...] = (
        dot(hv, w_two[:width, :], 1, 0) + dot(agg, w_two[width:, :], 1, 0)
    ).astype(BF)
    first = meta[0] == 0
    half = own.shape[0] // 2
    for part, left in enumerate((hv, agg)):
        grad = dot(left, cot[...], 0, 0)
        grad = grad.reshape(half, 2, own.shape[1], width)
        rows = pl.ds(part * half, half)
        own[rows] = jnp.where(first, grad[:, 0], grad[:, 1])
        sib[rows] = jnp.where(first, grad[:, 1], grad[:, 0]).astype(BF)


def two_sum_kernel(own, recv, out):
    n = own.shape[1]
    for x in range(NX):
        for z in range(NZ):
            total = own[x * NZ + z] + recv[x * NZ + z].astype(F32)
            out[z, pl.ds(x * n, n), :] = total.astype(BF)


def weight_grad_kernel(meta, *refs):
    feats, means = refs[:NX], refs[NX : 2 * NX]
    d_pre, own, sib = refs[2 * NX :]
    lanes = feats[0].shape[2]
    half = lanes // 2
    first = meta[0] == 0
    d_all = d_pre[...]
    bias = jnp.sum(d_all.astype(F32), axis=0, keepdims=True)
    tail = jnp.broadcast_to(bias, (16, bias.shape[1]))
    for d in range(NX):
        e = (NX - d) % NX
        for part, left in enumerate((feats[d], means[d])):
            grad = dot(left[...].reshape(-1, lanes), d_all, 0, 0)
            rows = pl.ds(part * half, half)
            own[e, rows, :] = jnp.where(first, grad[:half], grad[half:])
            sib[e, rows, :] = jnp.where(first, grad[half:], grad[:half])
        own[e, pl.ds(lanes, 16), :] = tail
        sib[e, pl.ds(lanes, 16), :] = tail


def core_sum_kernel(meta, own, recv, two, p0, p1, p2, p3):
    rows = own.shape[1]
    n = two.shape[1] // NX
    for e, out in enumerate((p0, p1, p2, p3)):
        out[:rows, :] = (own[e] + recv[e]).astype(BF)
        at = pl.multiple_of(lax.rem(meta[1] + e, NX) * n, n)
        total = two[0, pl.ds(at, n), :].astype(F32)
        for z in range(1, NZ):
            total = total + two[z, pl.ds(at, n), :].astype(F32)
        out[rows:, :] = total.astype(BF)


def four_sum(parts):
    p0, p1, p2, p3 = [p[...].astype(F32) for p in parts]
    return (p0 + p2) + (p1 + p3)


def x_sum_kernel(p0, p1, p2, p3, out):
    out[...] = four_sum((p0, p1, p2, p3)).astype(BF)


def y_sum_kernel(meta, p0, p1, p2, p3, grad, bias, two):
    total = four_sum((p0, p1, p2, p3))
    half = grad.shape[1]
    grad[0] = total[:half]
    grad[1] = total[half : 2 * half]
    bias[...] = total[2 * half : 2 * half + 1]
    n = two.shape[0]
    rows = total[2 * half + 16 :]
    mine = rows[:n]
    for y in range(1, NY):
        mine = jnp.where(meta[2] == y, rows[y * n : (y + 1) * n], mine)
    two[...] = mine


def all_to_all(value, axes):
    return lax.all_to_all(value, axes, split_axis=0, concat_axis=0, tiled=True)


def on_device(features, nbr_one, w_one, b_one, send_rows, nbr_slot, degree, w_two, cotangent):
    local = features[0]
    feats, group_nodes = local.shape
    fanout = nbr_one.shape[1]
    width = w_two.shape[1]
    owned = cotangent.shape[1]
    lanes = NC * feats
    per = CHIPS // STEPS
    core = lax.axis_index("core")
    x_at, y_at = lax.axis_index("x"), lax.axis_index("grp")
    meta = jnp.stack([core, x_at, y_at]).astype(jnp.int32)
    swap = lambda v: shift(v, "core", NC, 1)

    sibling = swap(local)
    w_all = lax.all_gather(w_one.reshape(-1, width), FEAT, axis=0, tiled=True)
    w_all = w_all.reshape(CHIPS * NC, 2, feats, width)

    deg_row = degree[0][None, :]
    cot = cotangent[0]
    slots = CHIPS * NC * NY * send_rows.shape[-1]
    d_table, d_self, counts = call(
        table_grad_kernel,
        (shape((slots, width), BF), shape((owned, width), F32), shape((slots, owned), BF)),
        [vmem()] * 4,
        (cot, w_two, nbr_slot, deg_row),
        "table_grad", us=3.0,
    )

    def exchange(rows):
        return all_to_all(rows.reshape(CHIPS * NC * NY, -1, width), ALL).reshape(-1, width)

    returned = exchange(d_table)

    tbl = call(
        lambda *refs: table_kernel(owned, *refs),
        shape((group_nodes, lanes), F32),
        [smem(), vmem(), vmem()],
        (meta, local, sibling),
        "node_table", us=6.0,
    )
    by_device = nbr_one[0].reshape(fanout, CHIPS, NC, owned)
    idx = lax.dynamic_index_in_dim(by_device, core, 2, keepdims=False)
    idx = idx.transpose(1, 0, 2).reshape(-1)
    mean_shape = shape((CHIPS, owned, lanes), BF)
    mean_per = CHIPS // MEAN_STEPS
    acc = [pltpu.VMEM((owned, lanes), F32)]
    us_per = idx.shape[0] * 1e-3 / MEAN_STEPS
    begun, mine = call(
        lambda *refs: first_mean_kernel(fanout, *refs),
        (mean_shape, mean_shape),
        [smem(), smem(), whole(tbl.shape), unread()],
        (meta, idx, tbl, d_table),
        "mean_first", acc, us_per * FIRST_MEANS, (FIRST_MEANS,),
        (pl.BlockSpec((mean_per, owned, lanes), lambda i: (i, 0, 0)), whole(mean_shape.shape)),
    )
    feats_here = all_to_all(mine, CHIP)
    last = MEAN_STEPS - FIRST_MEANS
    means = call(
        lambda *refs: last_mean_kernel(fanout, *refs),
        mean_shape,
        [smem(), whole(tbl.shape), unread(), unread()],
        (idx, tbl, begun, returned),
        "mean_last", acc, us_per * last, (last,),
        pl.BlockSpec((mean_per, owned, lanes), lambda i: (i + FIRST_MEANS, 0, 0)),
        {2: 0},
    )
    means_here = all_to_all(means, CHIP)

    left_spec = pl.BlockSpec((per, owned, lanes), lambda i: (i, 0, 0))

    def w_spec(part):
        return pl.BlockSpec((per * NC, 1, feats, width), lambda i: (i, part, 0, 0))

    self_part = call(
        self_kernel, shape((owned, width), F32), [left_spec, w_spec(0)], (feats_here, w_all),
        "self_part", us=4.0, grid=(STEPS,), out_specs=whole((owned, width)),
    )
    def over_x(value):
        by_x = value.reshape(NX, NZ, owned, lanes)
        pick = lambda d: lax.dynamic_index_in_dim(by_x, (x_at + d) % NX, 0, keepdims=False)
        return [shift(pick(d), "x", NX, d) if d else pick(0) for d in range(NX)]

    lefts = over_x(mine) + over_x(means)
    self_part, *lefts = lax.optimization_barrier((self_part, *lefts))

    send = send_rows[0, 0].reshape(1, -1)
    bias_row = b_one[None, :]
    ins = (self_part, bias_row, d_self, returned, send)
    outs = (shape((owned, width), BF), shape((owned, width), BF), shape((slots, width), BF))
    h_one, d_pre, outgoing = call(
        node_kernel,
        outs,
        [left_spec, w_spec(1)] + [whole(v.shape) for v in ins],
        (means_here, w_all, *ins),
        "node_update",
        [pltpu.VMEM((owned, width), F32)],
        us=4.0, grid=(STEPS,), out_specs=tuple(whole(o.shape) for o in outs),
    )
    d_pre_z = lax.all_gather(d_pre, "z", axis=0, tiled=True)
    table = exchange(outgoing)

    block_rows = 2 * width // (CHIPS * NC)
    emb, two_own, two_sib = call(
        layer_two_kernel,
        (
            shape((owned, width), BF),
            shape((CHIPS, block_rows, width), F32),
            shape((CHIPS, block_rows, width), BF),
        ),
        [smem()] + [vmem()] * 6,
        (meta, table, counts, deg_row, h_one, cot, w_two),
        "layer_two", us=3.0,
    )
    two_chip = call(
        two_sum_kernel,
        shape((NZ, NX * block_rows, width), BF),
        [vmem()] * 2,
        (two_own, swap(two_sib)),
        "two_sum",
    )
    d_pre_z, two_chip = lax.optimization_barrier((d_pre_z, two_chip))
    two_z = all_to_all(two_chip, "z")

    rows = 2 * feats + 16
    one_own, one_sib = call(
        weight_grad_kernel,
        (shape((NX, rows, width), F32), shape((NX, rows, width), F32)),
        [smem()] + [vmem()] * (2 * NX + 1),
        (meta, *lefts, d_pre_z),
        "weight_grad", us=15.0,
    )
    piece = shape((rows + block_rows, width), BF)
    sums = call(
        core_sum_kernel,
        (piece,) * NX,
        [smem()] + [vmem()] * 3,
        (meta, one_own, swap(one_sib), two_z),
        "core_sum", us=2.0,
    )
    got = [sums[0]] + [shift(sums[e], "x", NX, e) for e in range(1, NX)]
    total = call(x_sum_kernel, piece, [vmem()] * NX, tuple(got), "x_sum")
    got = [total] + [shift(total, "grp", NY, e) for e in range(1, NY)]
    grad_w_one, grad_b_one, grad_w_two = call(
        y_sum_kernel,
        (
            shape((2, feats, width), F32), shape((1, width), F32),
            shape((block_rows // NY, width), F32),
        ),
        [smem()] + [vmem()] * NY,
        (meta, *got),
        "y_sum",
    )
    return emb[None], grad_w_one, grad_b_one[0], grad_w_two


def solution(mesh):
    parts = Mesh(mesh.devices.reshape(NX, NZ, NC, NY), ALL)
    return jax.shard_map(
        on_device,
        mesh=parts,
        in_specs=(
            P("grp", FEAT, None),
            P("grp", None, None),
            P(None, FEAT, None),
            P(),
            P("grp", FEAT, None, None, None),
            P("grp", None, FEAT),
            P("grp", FEAT),
            P(),
            P("grp", FEAT, None),
        ),
        out_specs=(P("grp", FEAT, None), P(None, FEAT, None), P(), P(ALL, None)),
        check_vma=False,
    )
```

```python
import jax
import jax.numpy as jnp
from jax import lax
from jax.experimental import pallas as pl
from jax.experimental.pallas import tpu as pltpu
from jax.sharding import Mesh, PartitionSpec as P

BF = jnp.bfloat16
F32 = jnp.float32
NX, NZ, NC, NY = 4, 8, 2, 4
CHIPS = NX * NZ
STEPS = 4
MEAN_STEPS = 8
FIRST_MEANS = 2
FEAT = ("x", "z", "core")
CHIP = ("x", "z")
ALL = ("x", "z", "core", "grp")
LIMIT = 60 << 20


def vmem():
    return pl.BlockSpec()


def unread():
    return pl.BlockSpec(memory_space=pl.ANY)


def smem():
    return pl.BlockSpec(memory_space=pltpu.SMEM)


def call(body, outs, ins, args, name, scratch=(), us=1.0, grid=None, out_specs=None, alias=None):
    extra = {} if grid is None else {"grid": grid}
    if alias:
        extra["input_output_aliases"] = alias
    return pl.pallas_call(
        body,
        out_shape=outs,
        in_specs=ins,
        out_specs=jax.tree.map(lambda _: vmem(), outs) if out_specs is None else out_specs,
        scratch_shapes=list(scratch),
        cost_estimate=pl.CostEstimate(flops=0, bytes_accessed=int(us * 3.6e6), transcendentals=0),
        compiler_params=pltpu.CompilerParams(vmem_limit_bytes=LIMIT),
        name=name,
        **extra,
    )(*args)


def whole(dims):
    return pl.BlockSpec(dims, lambda i: (0,) * len(dims))


def shape(dims, kind):
    return jax.ShapeDtypeStruct(dims, kind)


def shift(value, axis, size, by):
    return lax.ppermute(value, axis, [(s, (s + by) % size) for s in range(size)])


def dot(a, b, ca, cb):
    return lax.dot_general(a, b, (((ca,), (cb,)), ((), ())), preferred_element_type=F32)


def table_kernel(owned, meta, own, sib, tbl):
    core = meta[0]
    first = core == 0
    def step(chip, carry):
        for c in range(NC):
            cols = pl.ds(pl.multiple_of((chip * NC + c) * owned, owned), owned)
            a, b = own[:, cols].astype(F32), sib[:, cols].astype(F32)
            pair = jnp.concatenate([jnp.where(first, a, b), jnp.where(first, b, a)], axis=0)
            tbl[cols, :] = pair.T
        return carry

    lax.fori_loop(0, CHIPS, step, 0, unroll=2)


def own_rows(core, tbl, mine):
    owned = mine.shape[1]

    def copy(chip, carry):
        at = pl.multiple_of((chip * NC + core) * owned, owned)
        mine[chip] = tbl[pl.ds(at, owned), :].astype(BF)
        return carry

    lax.fori_loop(0, CHIPS, copy, 0)


def mean_rows(fanout, first, idx, tbl, out, acc):
    owned = acc.shape[0]
    per = out.shape[0]

    def chunk(c, carry):
        base = ((first + pl.program_id(0)) * per + c) * (fanout * owned)

        def step(b, inner):
            for j in range(16):
                r = b * 16 + j
                rows = [tbl[pl.ds(idx[base + k * owned + r], 1), :] for k in range(fanout)]
                while len(rows) > 1:
                    rows = [
                        rows[i] + rows[i + 1] if i + 1 < len(rows) else rows[i]
                        for i in range(0, len(rows), 2)
                    ]
                acc[pl.ds(r, 1), :] = rows[0]
            return inner

        lax.fori_loop(0, owned // 16, step, 0)
        out[c] = (acc[...] / float(fanout)).astype(BF)
        return carry

    lax.fori_loop(0, per, chunk, 0)


def first_mean_kernel(fanout, meta, idx, tbl, after, out, mine, acc):
    @pl.when(pl.program_id(0) == 0)
    def _():
        own_rows(meta[0], tbl, mine)

    mean_rows(fanout, 0, idx, tbl, out, acc)


def last_mean_kernel(fanout, idx, tbl, begun, after, out, acc):
    mean_rows(fanout, FIRST_MEANS, idx, tbl, out, acc)


def by_row(deg_row, width):
    n = deg_row.shape[1]
    square = jnp.broadcast_to(deg_row[...].astype(F32), (n, n)).T
    return jnp.concatenate([square] * (width // n), axis=1)


def add_product(left, w, acc):
    per = left.shape[0]
    feats = w.shape[2]
    rows = w[...].reshape(per * NC * feats, w.shape[3])
    lhs = jnp.concatenate([left[i] for i in range(per)], axis=1)
    term = dot(lhs, rows, 1, 0)

    @pl.when(pl.program_id(0) == 0)
    def _():
        acc[...] = term

    @pl.when(pl.program_id(0) > 0)
    def _():
        acc[...] += term


def self_kernel(left, w, out):
    add_product(left, w, out)


def node_kernel(
    left, w, self_part, bias, d_self, returned, send, h_out, dpre_out, outgoing, acc
):
    add_product(left, w, acc)

    @pl.when(pl.program_id(0) == STEPS - 1)
    def _():
        pre = self_part[...] + acc[...] + bias[...]
        h = jnp.maximum(pre, 0.0).astype(BF)
        h_out[...] = h
        rows = lax.broadcasted_iota(jnp.int32, (pre.shape[0], send.shape[1]), 0)
        pick = (rows == send[...]).astype(F32).astype(BF)
        d_near = dot(pick, returned[...], 1, 0)
        dpre_out[...] = jnp.where(pre > 0.0, d_self[...] + d_near, 0.0).astype(BF)
        outgoing[...] = dot(pick, h, 0, 0).astype(BF)


def table_grad_kernel(cot, w_two, slot, deg_row, d_table, d_self, counts):
    width = cot.shape[1]
    k_two = slot.shape[1]
    live = lax.broadcasted_iota(jnp.int32, slot.shape[1:], 0) < deg_row[...]
    used = jnp.where(live, slot[0], -1)
    q = lax.broadcasted_iota(jnp.int32, counts.shape, 0)
    total = jnp.zeros(counts.shape, F32)
    for k in range(k_two):
        total = total + (q == used[k : k + 1, :]).astype(F32)
    ct = total.astype(BF)
    counts[...] = ct
    d_self[...] = dot(cot[...], w_two[:width, :], 1, 1)
    scaled = dot(cot[...], w_two[width:, :], 1, 1) / by_row(deg_row, width)
    hi = scaled.astype(BF)
    lo = (scaled - hi.astype(F32)).astype(BF)
    d_table[...] = (dot(ct, hi, 1, 0) + dot(ct, lo, 1, 0)).astype(BF)


def layer_two_kernel(meta, table, counts, deg_row, h, cot, w_two, emb, own, sib):
    width = cot.shape[1]
    agg = (dot(counts[...], table[...], 0, 0) / by_row(deg_row, width)).astype(BF)
    hv = h[...]
    emb[...] = (
        dot(hv, w_two[:width, :], 1, 0) + dot(agg, w_two[width:, :], 1, 0)
    ).astype(BF)
    first = meta[0] == 0
    half = own.shape[0] // 2
    for part, left in enumerate((hv, agg)):
        grad = dot(left, cot[...], 0, 0)
        grad = grad.reshape(half, 2, own.shape[1], width)
        rows = pl.ds(part * half, half)
        own[rows] = jnp.where(first, grad[:, 0], grad[:, 1])
        sib[rows] = jnp.where(first, grad[:, 1], grad[:, 0]).astype(BF)


def weight_grad_kernel(meta, *refs):
    feats, means = refs[:NX], refs[NX : 2 * NX]
    d_pre, own, sib = refs[2 * NX :]
    lanes = feats[0].shape[2]
    half = lanes // 2
    first = meta[0] == 0
    d_all = d_pre[...]
    bias = jnp.sum(d_all.astype(F32), axis=0, keepdims=True)
    tail = jnp.broadcast_to(bias, (16, bias.shape[1]))
    for d in range(NX):
        e = (NX - d) % NX
        for part, left in enumerate((feats[d], means[d])):
            grad = dot(left[...].reshape(-1, lanes), d_all, 0, 0)
            rows = pl.ds(part * half, half)
            own[e, rows, :] = jnp.where(first, grad[:half], grad[half:])
            sib[e, rows, :] = jnp.where(first, grad[half:], grad[:half])
        own[e, pl.ds(lanes, 16), :] = tail
        sib[e, pl.ds(lanes, 16), :] = tail


def core_sum_kernel(meta, own, recv, two_own, two_recv, p0, p1, p2, p3):
    rows = own.shape[1]
    for e, out in enumerate((p0, p1, p2, p3)):
        out[:rows, :] = (own[e] + recv[e]).astype(BF)
        x = lax.rem(meta[1] + e, NX)
        out[rows:, :] = (two_own[x] + two_recv[x].astype(F32)).astype(BF)


def four_sum(parts):
    p0, p1, p2, p3 = [p[...].astype(F32) for p in parts]
    return (p0 + p2) + (p1 + p3)


def x_sum_kernel(p0, p1, p2, p3, one, two):
    total = four_sum((p0, p1, p2, p3)).astype(BF)
    rows = one.shape[0]
    one[...] = total[:rows]
    two[...] = total[rows:]


def y_sum_kernel(p0, p1, p2, p3, grad, bias):
    total = four_sum((p0, p1, p2, p3))
    half = grad.shape[1]
    grad[0] = total[:half]
    grad[1] = total[half : 2 * half]
    bias[...] = total[2 * half : 2 * half + 1]


def all_to_all(value, axes):
    return lax.all_to_all(value, axes, split_axis=0, concat_axis=0, tiled=True)


def on_device(features, nbr_one, w_one, b_one, send_rows, nbr_slot, degree, w_two, cotangent):
    local = features[0]
    feats, group_nodes = local.shape
    fanout = nbr_one.shape[1]
    width = w_two.shape[1]
    owned = cotangent.shape[1]
    lanes = NC * feats
    per = CHIPS // STEPS
    core = lax.axis_index("core")
    x_at, y_at = lax.axis_index("x"), lax.axis_index("grp")
    meta = jnp.stack([core, x_at, y_at]).astype(jnp.int32)
    swap = lambda v: shift(v, "core", NC, 1)

    sibling = swap(local)
    w_all = lax.all_gather(w_one.reshape(-1, width), FEAT, axis=0, tiled=True)
    w_all = w_all.reshape(CHIPS * NC, 2, feats, width)

    deg_row = degree[0][None, :]
    cot = cotangent[0]
    slots = CHIPS * NC * NY * send_rows.shape[-1]
    d_table, d_self, counts = call(
        table_grad_kernel,
        (shape((slots, width), BF), shape((owned, width), F32), shape((slots, owned), BF)),
        [vmem()] * 4,
        (cot, w_two, nbr_slot, deg_row),
        "table_grad", us=3.0,
    )

    def exchange(rows):
        return all_to_all(rows.reshape(CHIPS * NC * NY, -1, width), ALL).reshape(-1, width)

    returned = exchange(d_table)

    tbl = call(
        lambda *refs: table_kernel(owned, *refs),
        shape((group_nodes, lanes), F32),
        [smem(), vmem(), vmem()],
        (meta, local, sibling),
        "node_table", us=6.0,
    )
    by_device = nbr_one[0].reshape(fanout, CHIPS, NC, owned)
    idx = lax.dynamic_index_in_dim(by_device, core, 2, keepdims=False)
    idx = idx.transpose(1, 0, 2).reshape(-1)
    mean_shape = shape((CHIPS, owned, lanes), BF)
    mean_per = CHIPS // MEAN_STEPS
    acc = [pltpu.VMEM((owned, lanes), F32)]
    us_per = idx.shape[0] * 1e-3 / MEAN_STEPS
    begun, mine = call(
        lambda *refs: first_mean_kernel(fanout, *refs),
        (mean_shape, mean_shape),
        [smem(), smem(), whole(tbl.shape), unread()],
        (meta, idx, tbl, d_table),
        "mean_first", acc, us_per * FIRST_MEANS, (FIRST_MEANS,),
        (pl.BlockSpec((mean_per, owned, lanes), lambda i: (i, 0, 0)), whole(mean_shape.shape)),
    )
    def over_x(value):
        by_x = value.reshape(NX, NZ, owned, lanes)
        pick = lambda d: lax.dynamic_index_in_dim(by_x, (x_at + d) % NX, 0, keepdims=False)
        return [shift(pick(d), "x", NX, d) if d else pick(0) for d in range(NX)]

    feats_here = all_to_all(mine, CHIP)
    lefts = over_x(mine)
    last = MEAN_STEPS - FIRST_MEANS
    means = call(
        lambda *refs: last_mean_kernel(fanout, *refs),
        mean_shape,
        [smem(), whole(tbl.shape), unread(), unread()],
        (idx, tbl, begun, returned),
        "mean_last", acc, us_per * last, (last,),
        pl.BlockSpec((mean_per, owned, lanes), lambda i: (i + FIRST_MEANS, 0, 0)),
        {2: 0},
    )
    means, *lefts = lax.optimization_barrier((means, *lefts))
    means_here = all_to_all(means, CHIP)

    left_spec = pl.BlockSpec((per, owned, lanes), lambda i: (i, 0, 0))

    def w_spec(part):
        return pl.BlockSpec((per * NC, 1, feats, width), lambda i: (i, part, 0, 0))

    self_part = call(
        self_kernel, shape((owned, width), F32), [left_spec, w_spec(0)], (feats_here, w_all),
        "self_part", us=4.0, grid=(STEPS,), out_specs=whole((owned, width)),
    )
    lefts = lefts + over_x(means)
    self_part, *lefts = lax.optimization_barrier((self_part, *lefts))

    send = send_rows[0, 0].reshape(1, -1)
    bias_row = b_one[None, :]
    ins = (self_part, bias_row, d_self, returned, send)
    outs = (shape((owned, width), BF), shape((owned, width), BF), shape((slots, width), BF))
    h_one, d_pre, outgoing = call(
        node_kernel,
        outs,
        [left_spec, w_spec(1)] + [whole(v.shape) for v in ins],
        (means_here, w_all, *ins),
        "node_update",
        [pltpu.VMEM((owned, width), F32)],
        us=4.0, grid=(STEPS,), out_specs=tuple(whole(o.shape) for o in outs),
    )
    d_pre_z = lax.all_gather(d_pre, "z", axis=0, tiled=True)
    table = exchange(outgoing)

    block_rows = 2 * width // (CHIPS * NC)
    emb, two_own, two_sib = call(
        layer_two_kernel,
        (
            shape((owned, width), BF),
            shape((CHIPS, block_rows, width), F32),
            shape((CHIPS, block_rows, width), BF),
        ),
        [smem()] + [vmem()] * 6,
        (meta, table, counts, deg_row, h_one, cot, w_two),
        "layer_two", us=3.0,
    )
    d_pre_z, two_sib = lax.optimization_barrier((d_pre_z, two_sib))
    two_recv = swap(two_sib)

    rows = 2 * feats + 16
    one_own, one_sib = call(
        weight_grad_kernel,
        (shape((NX, rows, width), F32), shape((NX, rows, width), F32)),
        [smem()] + [vmem()] * (2 * NX + 1),
        (meta, *lefts, d_pre_z),
        "weight_grad", us=15.0,
    )
    two_rows = NZ * block_rows
    sums = call(
        core_sum_kernel,
        (shape((rows + two_rows, width), BF),) * NX,
        [smem()] + [vmem()] * 4,
        (
            meta, one_own, swap(one_sib), two_own.reshape(NX, two_rows, width),
            two_recv.reshape(NX, two_rows, width),
        ),
        "core_sum", us=2.0,
    )
    got = [sums[0]] + [shift(sums[e], "x", NX, e) for e in range(1, NX)]
    total, two = call(
        x_sum_kernel, (shape((rows, width), BF), shape((two_rows, width), BF)), [vmem()] * NX,
        tuple(got), "x_sum",
    )
    two_last = all_to_all(two.reshape(NZ * NY, -1, width), ("z", "grp"))
    grad_w_two = jnp.sum(two_last.astype(F32), axis=0)
    got = [total] + [shift(total, "grp", NY, e) for e in range(1, NY)]
    grad_w_one, grad_b_one = call(
        y_sum_kernel,
        (shape((2, feats, width), F32), shape((1, width), F32)),
        [vmem()] * NY,
        tuple(got),
        "y_sum",
    )
    return emb[None], grad_w_one, grad_b_one[0], grad_w_two


def solution(mesh):
    parts = Mesh(mesh.devices.reshape(NX, NZ, NC, NY), ALL)
    return jax.shard_map(
        on_device,
        mesh=parts,
        in_specs=(
            P("grp", FEAT, None),
            P("grp", None, None),
            P(None, FEAT, None),
            P(),
            P("grp", FEAT, None, None, None),
            P("grp", None, FEAT),
            P("grp", FEAT),
            P(),
            P("grp", FEAT, None),
        ),
        out_specs=(P("grp", FEAT, None), P(None, FEAT, None), P(), P(ALL, None)),
        check_vma=False,
    )
```

```python
import jax
import jax.numpy as jnp
from jax import lax
from jax.experimental import pallas as pl
from jax.experimental.pallas import tpu as pltpu
from jax.sharding import Mesh, PartitionSpec as P

BF = jnp.bfloat16
F32 = jnp.float32
NX, NZ, NC, NY = 4, 8, 2, 4
CHIPS = NX * NZ
STEPS = 4
MEAN_STEPS = 8
FIRST_MEANS = 3
FEAT = ("x", "z", "core")
CHIP = ("x", "z")
ALL = ("x", "z", "core", "grp")
LIMIT = 60 << 20


def vmem():
    return pl.BlockSpec()


def unread():
    return pl.BlockSpec(memory_space=pl.ANY)


def smem():
    return pl.BlockSpec(memory_space=pltpu.SMEM)


def call(body, outs, ins, args, name, scratch=(), us=1.0, grid=None, out_specs=None, alias=None):
    extra = {} if grid is None else {"grid": grid}
    if alias:
        extra["input_output_aliases"] = alias
    return pl.pallas_call(
        body,
        out_shape=outs,
        in_specs=ins,
        out_specs=jax.tree.map(lambda _: vmem(), outs) if out_specs is None else out_specs,
        scratch_shapes=list(scratch),
        cost_estimate=pl.CostEstimate(flops=0, bytes_accessed=int(us * 3.6e6), transcendentals=0),
        compiler_params=pltpu.CompilerParams(vmem_limit_bytes=LIMIT),
        name=name,
        **extra,
    )(*args)


def whole(dims):
    return pl.BlockSpec(dims, lambda i: (0,) * len(dims))


def shape(dims, kind):
    return jax.ShapeDtypeStruct(dims, kind)


def shift(value, axis, size, by):
    return lax.ppermute(value, axis, [(s, (s + by) % size) for s in range(size)])


def dot(a, b, ca, cb):
    return lax.dot_general(a, b, (((ca,), (cb,)), ((), ())), preferred_element_type=F32)


def make_table(owned, core, own, sib, tbl):
    first = core == 0
    def step(chip, carry):
        for c in range(NC):
            cols = pl.ds(pl.multiple_of((chip * NC + c) * owned, owned), owned)
            a, b = own[:, cols].astype(F32), sib[:, cols].astype(F32)
            pair = jnp.concatenate([jnp.where(first, a, b), jnp.where(first, b, a)], axis=0)
            tbl[cols, :] = pair.T
        return carry

    lax.fori_loop(0, CHIPS, step, 0, unroll=2)


def own_rows(core, tbl, mine):
    owned = mine.shape[1]

    def copy(chip, carry):
        at = pl.multiple_of((chip * NC + core) * owned, owned)
        mine[chip] = tbl[pl.ds(at, owned), :].astype(BF)
        return carry

    lax.fori_loop(0, CHIPS, copy, 0)


def mean_rows(fanout, first, idx, tbl, out, acc):
    owned = acc.shape[0]
    per = out.shape[0]

    def chunk(c, carry):
        base = ((first + pl.program_id(0)) * per + c) * (fanout * owned)

        def step(b, inner):
            for j in range(16):
                r = b * 16 + j
                rows = [tbl[pl.ds(idx[base + k * owned + r], 1), :] for k in range(fanout)]
                while len(rows) > 1:
                    rows = [
                        rows[i] + rows[i + 1] if i + 1 < len(rows) else rows[i]
                        for i in range(0, len(rows), 2)
                    ]
                acc[pl.ds(r, 1), :] = rows[0]
            return inner

        lax.fori_loop(0, owned // 16, step, 0)
        out[c] = (acc[...] / float(fanout)).astype(BF)
        return carry

    lax.fori_loop(0, per, chunk, 0)


def first_mean_kernel(fanout, meta, idx, own, sib, after, out, mine, tbl, acc):
    @pl.when(pl.program_id(0) == 0)
    def _():
        make_table(mine.shape[1], meta[0], own, sib, tbl)
        own_rows(meta[0], tbl, mine)

    mean_rows(fanout, 0, idx, tbl, out, acc)


def last_mean_kernel(fanout, idx, tbl, begun, after, out, acc):
    mean_rows(fanout, FIRST_MEANS, idx, tbl, out, acc)


def by_row(deg_row, width):
    n = deg_row.shape[1]
    square = jnp.broadcast_to(deg_row[...].astype(F32), (n, n)).T
    return jnp.concatenate([square] * (width // n), axis=1)


def add_product(left, w, acc):
    per = left.shape[0]
    feats = w.shape[2]
    rows = w[...].reshape(per * NC * feats, w.shape[3])
    lhs = jnp.concatenate([left[i] for i in range(per)], axis=1)
    term = dot(lhs, rows, 1, 0)

    @pl.when(pl.program_id(0) == 0)
    def _():
        acc[...] = term

    @pl.when(pl.program_id(0) > 0)
    def _():
        acc[...] += term


def self_kernel(left, w, out):
    add_product(left, w, out)


def node_kernel(
    left, w, self_part, bias, d_self, returned, send, h_out, dpre_out, outgoing, acc
):
    add_product(left, w, acc)

    @pl.when(pl.program_id(0) == STEPS - 1)
    def _():
        pre = self_part[...] + acc[...] + bias[...]
        h = jnp.maximum(pre, 0.0).astype(BF)
        h_out[...] = h
        rows = lax.broadcasted_iota(jnp.int32, (pre.shape[0], send.shape[1]), 0)
        pick = (rows == send[...]).astype(F32).astype(BF)
        d_near = dot(pick, returned[...], 1, 0)
        dpre_out[...] = jnp.where(pre > 0.0, d_self[...] + d_near, 0.0).astype(BF)
        outgoing[...] = dot(pick, h, 0, 0).astype(BF)


def table_grad_kernel(cot, w_two, slot, deg_row, d_table, d_self, counts):
    width = cot.shape[1]
    k_two = slot.shape[1]
    live = lax.broadcasted_iota(jnp.int32, slot.shape[1:], 0) < deg_row[...]
    used = jnp.where(live, slot[0], -1)
    q = lax.broadcasted_iota(jnp.int32, counts.shape, 0)
    total = jnp.zeros(counts.shape, F32)
    for k in range(k_two):
        total = total + (q == used[k : k + 1, :]).astype(F32)
    ct = total.astype(BF)
    counts[...] = ct
    d_self[...] = dot(cot[...], w_two[:width, :], 1, 1)
    scaled = dot(cot[...], w_two[width:, :], 1, 1) / by_row(deg_row, width)
    hi = scaled.astype(BF)
    lo = (scaled - hi.astype(F32)).astype(BF)
    d_table[...] = (dot(ct, hi, 1, 0) + dot(ct, lo, 1, 0)).astype(BF)


def layer_two_kernel(meta, table, counts, deg_row, h, cot, w_two, emb, own, sib):
    width = cot.shape[1]
    agg = (dot(counts[...], table[...], 0, 0) / by_row(deg_row, width)).astype(BF)
    hv = h[...]
    emb[...] = (
        dot(hv, w_two[:width, :], 1, 0) + dot(agg, w_two[width:, :], 1, 0)
    ).astype(BF)
    first = meta[0] == 0
    half = own.shape[0] // 2
    for part, left in enumerate((hv, agg)):
        grad = dot(left, cot[...], 0, 0)
        grad = grad.reshape(half, 2, own.shape[1], width)
        rows = pl.ds(part * half, half)
        own[rows] = jnp.where(first, grad[:, 0], grad[:, 1])
        sib[rows] = jnp.where(first, grad[:, 1], grad[:, 0]).astype(BF)


def weight_grad_kernel(meta, *refs):
    feats, means = refs[:NX], refs[NX : 2 * NX]
    d_pre, own, sib = refs[2 * NX :]
    lanes = feats[0].shape[2]
    half = lanes // 2
    first = meta[0] == 0
    d_all = d_pre[...]
    bias = jnp.sum(d_all.astype(F32), axis=0, keepdims=True)
    tail = jnp.broadcast_to(bias, (16, bias.shape[1]))
    for d in range(NX):
        e = (NX - d) % NX
        for part, left in enumerate((feats[d], means[d])):
            grad = dot(left[...].reshape(-1, lanes), d_all, 0, 0)
            rows = pl.ds(part * half, half)
            own[e, rows, :] = jnp.where(first, grad[:half], grad[half:])
            sib[e, rows, :] = jnp.where(first, grad[half:], grad[:half])
        own[e, pl.ds(lanes, 16), :] = tail
        sib[e, pl.ds(lanes, 16), :] = tail


def core_sum_kernel(meta, own, recv, two_own, two_recv, p0, p1, p2, p3):
    rows = own.shape[1]
    for e, out in enumerate((p0, p1, p2, p3)):
        out[:rows, :] = (own[e] + recv[e]).astype(BF)
        x = lax.rem(meta[1] + e, NX)
        out[rows:, :] = (two_own[x] + two_recv[x].astype(F32)).astype(BF)


def four_sum(parts):
    p0, p1, p2, p3 = [p[...].astype(F32) for p in parts]
    return (p0 + p2) + (p1 + p3)


def x_sum_kernel(p0, p1, p2, p3, one, two):
    total = four_sum((p0, p1, p2, p3))
    rows = one.shape[0]
    one[...] = total[:rows].astype(BF)
    n = two.shape[1]
    for i in range(two.shape[0]):
        two[i] = total[rows + i * n : rows + (i + 1) * n]


def y_sum_kernel(p0, p1, p2, p3, grad, bias):
    total = four_sum((p0, p1, p2, p3))
    half = grad.shape[1]
    grad[0] = total[:half]
    grad[1] = total[half : 2 * half]
    bias[...] = total[2 * half : 2 * half + 1]


def all_to_all(value, axes):
    return lax.all_to_all(value, axes, split_axis=0, concat_axis=0, tiled=True)


def on_device(features, nbr_one, w_one, b_one, send_rows, nbr_slot, degree, w_two, cotangent):
    local = features[0]
    feats, group_nodes = local.shape
    fanout = nbr_one.shape[1]
    width = w_two.shape[1]
    owned = cotangent.shape[1]
    lanes = NC * feats
    per = CHIPS // STEPS
    core = lax.axis_index("core")
    x_at, y_at = lax.axis_index("x"), lax.axis_index("grp")
    meta = jnp.stack([core, x_at, y_at]).astype(jnp.int32)
    swap = lambda v: shift(v, "core", NC, 1)

    sibling = swap(local)
    w_all = lax.all_gather(w_one.reshape(-1, width), FEAT, axis=0, tiled=True)
    w_all = w_all.reshape(CHIPS * NC, 2, feats, width)

    deg_row = degree[0][None, :]
    cot = cotangent[0]
    slots = CHIPS * NC * NY * send_rows.shape[-1]
    d_table, d_self, counts = call(
        table_grad_kernel,
        (shape((slots, width), BF), shape((owned, width), F32), shape((slots, owned), BF)),
        [vmem()] * 4,
        (cot, w_two, nbr_slot, deg_row),
        "table_grad", us=3.0,
    )

    def exchange(rows):
        return all_to_all(rows.reshape(CHIPS * NC * NY, -1, width), ALL).reshape(-1, width)

    returned = exchange(d_table)

    by_device = nbr_one[0].reshape(fanout, CHIPS, NC, owned)
    idx = lax.dynamic_index_in_dim(by_device, core, 2, keepdims=False)
    idx = idx.transpose(1, 0, 2).reshape(-1)
    mean_shape = shape((CHIPS, owned, lanes), BF)
    mean_per = CHIPS // MEAN_STEPS
    acc = [pltpu.VMEM((owned, lanes), F32)]
    us_per = idx.shape[0] * 1e-3 / MEAN_STEPS
    table_shape = shape((group_nodes, lanes), F32)
    begun, mine, tbl = call(
        lambda *refs: first_mean_kernel(fanout, *refs),
        (mean_shape, mean_shape, table_shape),
        [smem(), smem(), whole(local.shape), whole(local.shape), unread()],
        (meta, idx, local, sibling, d_table),
        "mean_first", acc, us_per * FIRST_MEANS + 5.0, (FIRST_MEANS,),
        (
            pl.BlockSpec((mean_per, owned, lanes), lambda i: (i, 0, 0)),
            whole(mean_shape.shape), whole(table_shape.shape),
        ),
    )
    def over_x(value):
        by_x = value.reshape(NX, NZ, owned, lanes)
        pick = lambda d: lax.dynamic_index_in_dim(by_x, (x_at + d) % NX, 0, keepdims=False)
        return [shift(pick(d), "x", NX, d) if d else pick(0) for d in range(NX)]

    feats_here = all_to_all(mine, CHIP)
    lefts = over_x(mine)
    last = MEAN_STEPS - FIRST_MEANS
    means = call(
        lambda *refs: last_mean_kernel(fanout, *refs),
        mean_shape,
        [smem(), whole(tbl.shape), unread(), unread()],
        (idx, tbl, begun, returned),
        "mean_last", acc, us_per * last, (last,),
        pl.BlockSpec((mean_per, owned, lanes), lambda i: (i + FIRST_MEANS, 0, 0)),
        {2: 0},
    )
    means, *lefts = lax.optimization_barrier((means, *lefts))
    means_here = all_to_all(means, CHIP)

    left_spec = pl.BlockSpec((per, owned, lanes), lambda i: (i, 0, 0))

    def w_spec(part):
        return pl.BlockSpec((per * NC, 1, feats, width), lambda i: (i, part, 0, 0))

    self_part = call(
        self_kernel, shape((owned, width), F32), [left_spec, w_spec(0)], (feats_here, w_all),
        "self_part", us=4.0, grid=(STEPS,), out_specs=whole((owned, width)),
    )
    lefts = lefts + over_x(means)
    self_part, *lefts = lax.optimization_barrier((self_part, *lefts))

    send = send_rows[0, 0].reshape(1, -1)
    bias_row = b_one[None, :]
    ins = (self_part, bias_row, d_self, returned, send)
    outs = (shape((owned, width), BF), shape((owned, width), BF), shape((slots, width), BF))
    h_one, d_pre, outgoing = call(
        node_kernel,
        outs,
        [left_spec, w_spec(1)] + [whole(v.shape) for v in ins],
        (means_here, w_all, *ins),
        "node_update",
        [pltpu.VMEM((owned, width), F32)],
        us=4.0, grid=(STEPS,), out_specs=tuple(whole(o.shape) for o in outs),
    )
    d_pre_z = lax.all_gather(d_pre, "z", axis=0, tiled=True)
    table = exchange(outgoing)

    block_rows = 2 * width // (CHIPS * NC)
    emb, two_own, two_sib = call(
        layer_two_kernel,
        (
            shape((owned, width), BF),
            shape((CHIPS, block_rows, width), F32),
            shape((CHIPS, block_rows, width), BF),
        ),
        [smem()] + [vmem()] * 6,
        (meta, table, counts, deg_row, h_one, cot, w_two),
        "layer_two", us=3.0,
    )
    d_pre_z, two_sib = lax.optimization_barrier((d_pre_z, two_sib))
    two_recv = swap(two_sib)

    rows = 2 * feats + 16
    one_own, one_sib = call(
        weight_grad_kernel,
        (shape((NX, rows, width), F32), shape((NX, rows, width), F32)),
        [smem()] + [vmem()] * (2 * NX + 1),
        (meta, *lefts, d_pre_z),
        "weight_grad", us=15.0,
    )
    two_rows = NZ * block_rows
    sums = call(
        core_sum_kernel,
        (shape((rows + two_rows, width), BF),) * NX,
        [smem()] + [vmem()] * 4,
        (
            meta, one_own, swap(one_sib), two_own.reshape(NX, two_rows, width),
            two_recv.reshape(NX, two_rows, width),
        ),
        "core_sum", us=2.0,
    )
    got = [sums[0]] + [shift(sums[e], "x", NX, e) for e in range(1, NX)]
    total, two = call(
        x_sum_kernel, (shape((rows, width), BF), shape((NZ * NY, block_rows // NY, width), F32)),
        [vmem()] * NX,
        tuple(got), "x_sum",
    )
    grad_w_two = jnp.sum(all_to_all(two, ("z", "grp")), axis=0)
    got = [total] + [shift(total, "grp", NY, e) for e in range(1, NY)]
    grad_w_one, grad_b_one = call(
        y_sum_kernel,
        (shape((2, feats, width), F32), shape((1, width), F32)),
        [vmem()] * NY,
        tuple(got),
        "y_sum",
    )
    return emb[None], grad_w_one, grad_b_one[0], grad_w_two


def solution(mesh):
    parts = Mesh(mesh.devices.reshape(NX, NZ, NC, NY), ALL)
    return jax.shard_map(
        on_device,
        mesh=parts,
        in_specs=(
            P("grp", FEAT, None),
            P("grp", None, None),
            P(None, FEAT, None),
            P(),
            P("grp", FEAT, None, None, None),
            P("grp", None, FEAT),
            P("grp", FEAT),
            P(),
            P("grp", FEAT, None),
        ),
        out_specs=(P("grp", FEAT, None), P(None, FEAT, None), P(), P(ALL, None)),
        check_vma=False,
    )
```

```python
import jax
import jax.numpy as jnp
from jax import lax
from jax.experimental import pallas as pl
from jax.experimental.pallas import tpu as pltpu
from jax.sharding import Mesh, PartitionSpec as P

BF = jnp.bfloat16
F32 = jnp.float32
NX, NZ, NC, NY = 4, 8, 2, 4
CHIPS = NX * NZ
STEPS = 4
MEAN_STEPS = 8
FIRST_MEANS = 2
FEAT = ("x", "z", "core")
CHIP = ("x", "z")
ALL = ("x", "z", "core", "grp")
LIMIT = 60 << 20


def vmem():
    return pl.BlockSpec()


def unread():
    return pl.BlockSpec(memory_space=pl.ANY)


def smem():
    return pl.BlockSpec(memory_space=pltpu.SMEM)


def call(body, outs, ins, args, name, scratch=(), us=1.0, grid=None, out_specs=None, alias=None):
    extra = {} if grid is None else {"grid": grid}
    if alias:
        extra["input_output_aliases"] = alias
    return pl.pallas_call(
        body,
        out_shape=outs,
        in_specs=ins,
        out_specs=jax.tree.map(lambda _: vmem(), outs) if out_specs is None else out_specs,
        scratch_shapes=list(scratch),
        cost_estimate=pl.CostEstimate(flops=0, bytes_accessed=int(us * 3.6e6), transcendentals=0),
        compiler_params=pltpu.CompilerParams(vmem_limit_bytes=LIMIT),
        name=name,
        **extra,
    )(*args)


def whole(dims):
    return pl.BlockSpec(dims, lambda i: (0,) * len(dims))


def shape(dims, kind):
    return jax.ShapeDtypeStruct(dims, kind)


def shift(value, axis, size, by):
    return lax.ppermute(value, axis, [(s, (s + by) % size) for s in range(size)])


def dot(a, b, ca, cb):
    return lax.dot_general(a, b, (((ca,), (cb,)), ((), ())), preferred_element_type=F32)


def make_table(owned, core, own, sib, tbl):
    first = core == 0
    def step(chip, carry):
        for c in range(NC):
            cols = pl.ds(pl.multiple_of((chip * NC + c) * owned, owned), owned)
            a, b = own[:, cols].astype(F32), sib[:, cols].astype(F32)
            pair = jnp.concatenate([jnp.where(first, a, b), jnp.where(first, b, a)], axis=0)
            tbl[cols, :] = pair.T
        return carry

    lax.fori_loop(0, CHIPS, step, 0, unroll=2)


def own_rows(core, tbl, mine):
    owned = mine.shape[1]

    def copy(chip, carry):
        at = pl.multiple_of((chip * NC + core) * owned, owned)
        mine[chip] = tbl[pl.ds(at, owned), :].astype(BF)
        return carry

    lax.fori_loop(0, CHIPS, copy, 0)


def mean_rows(fanout, first, idx, tbl, out, acc):
    owned = acc.shape[0]
    per = out.shape[0]

    def chunk(c, carry):
        base = ((first + pl.program_id(0)) * per + c) * (fanout * owned)

        def step(b, inner):
            for j in range(16):
                r = b * 16 + j
                rows = [tbl[pl.ds(idx[base + k * owned + r], 1), :] for k in range(fanout)]
                while len(rows) > 1:
                    rows = [
                        rows[i] + rows[i + 1] if i + 1 < len(rows) else rows[i]
                        for i in range(0, len(rows), 2)
                    ]
                acc[pl.ds(r, 1), :] = rows[0]
            return inner

        lax.fori_loop(0, owned // 16, step, 0)
        out[c] = (acc[...] / float(fanout)).astype(BF)
        return carry

    lax.fori_loop(0, per, chunk, 0)


def first_mean_kernel(fanout, meta, idx, own, sib, after, out, mine, tbl, acc):
    @pl.when(pl.program_id(0) == 0)
    def _():
        make_table(mine.shape[1], meta[0], own, sib, tbl)
        own_rows(meta[0], tbl, mine)

    mean_rows(fanout, 0, idx, tbl, out, acc)


def last_mean_kernel(fanout, idx, tbl, begun, after, out, acc):
    mean_rows(fanout, FIRST_MEANS, idx, tbl, out, acc)


def by_row(deg_row, width):
    n = deg_row.shape[1]
    square = jnp.broadcast_to(deg_row[...].astype(F32), (n, n)).T
    return jnp.concatenate([square] * (width // n), axis=1)


def add_product(left, w, acc):
    per = left.shape[0]
    feats = w.shape[2]
    rows = w[...].reshape(per * NC * feats, w.shape[3])
    lhs = jnp.concatenate([left[i] for i in range(per)], axis=1)
    term = dot(lhs, rows, 1, 0)

    @pl.when(pl.program_id(0) == 0)
    def _():
        acc[...] = term

    @pl.when(pl.program_id(0) > 0)
    def _():
        acc[...] += term


def self_kernel(left, w, out):
    add_product(left, w, out)


def node_kernel(
    left, w, self_part, bias, d_self, returned, send, h_out, dpre_out, outgoing, acc
):
    add_product(left, w, acc)

    @pl.when(pl.program_id(0) == STEPS - 1)
    def _():
        pre = self_part[...] + acc[...] + bias[...]
        h = jnp.maximum(pre, 0.0).astype(BF)
        h_out[...] = h
        rows = lax.broadcasted_iota(jnp.int32, (pre.shape[0], send.shape[1]), 0)
        pick = (rows == send[...]).astype(F32).astype(BF)
        d_near = dot(pick, returned[...], 1, 0)
        dpre_out[...] = jnp.where(pre > 0.0, d_self[...] + d_near, 0.0).astype(BF)
        outgoing[...] = dot(pick, h, 0, 0).astype(BF)


def table_grad_kernel(cot, w_two, slot, deg_row, d_table, d_self, counts):
    width = cot.shape[1]
    k_two = slot.shape[1]
    live = lax.broadcasted_iota(jnp.int32, slot.shape[1:], 0) < deg_row[...]
    used = jnp.where(live, slot[0], -1)
    q = lax.broadcasted_iota(jnp.int32, counts.shape, 0)
    total = jnp.zeros(counts.shape, F32)
    for k in range(k_two):
        total = total + (q == used[k : k + 1, :]).astype(F32)
    ct = total.astype(BF)
    counts[...] = ct
    d_self[...] = dot(cot[...], w_two[:width, :], 1, 1)
    scaled = dot(cot[...], w_two[width:, :], 1, 1) / by_row(deg_row, width)
    hi = scaled.astype(BF)
    lo = (scaled - hi.astype(F32)).astype(BF)
    d_table[...] = (dot(ct, hi, 1, 0) + dot(ct, lo, 1, 0)).astype(BF)


def layer_two_kernel(meta, table, counts, deg_row, h, cot, w_two, emb, own, sib):
    width = cot.shape[1]
    agg = (dot(counts[...], table[...], 0, 0) / by_row(deg_row, width)).astype(BF)
    hv = h[...]
    emb[...] = (
        dot(hv, w_two[:width, :], 1, 0) + dot(agg, w_two[width:, :], 1, 0)
    ).astype(BF)
    first = meta[0] == 0
    half = own.shape[0] // 2
    for part, left in enumerate((hv, agg)):
        grad = dot(left, cot[...], 0, 0)
        grad = grad.reshape(half, 2, own.shape[1], width)
        rows = pl.ds(part * half, half)
        own[rows] = jnp.where(first, grad[:, 0], grad[:, 1])
        sib[rows] = jnp.where(first, grad[:, 1], grad[:, 0]).astype(BF)


def weight_grad_kernel(meta, *refs):
    feats, means = refs[:NX], refs[NX : 2 * NX]
    d_pre, own, sib = refs[2 * NX :]
    lanes = feats[0].shape[2]
    half = lanes // 2
    first = meta[0] == 0
    d_all = d_pre[...]
    bias = jnp.sum(d_all.astype(F32), axis=0, keepdims=True)
    tail = jnp.broadcast_to(bias, (16, bias.shape[1]))
    for d in range(NX):
        e = (NX - d) % NX
        for part, left in enumerate((feats[d], means[d])):
            grad = dot(left[...].reshape(-1, lanes), d_all, 0, 0)
            rows = pl.ds(part * half, half)
            own[e, rows, :] = jnp.where(first, grad[:half], grad[half:])
            sib[e, rows, :] = jnp.where(first, grad[half:], grad[:half])
        own[e, pl.ds(lanes, 16), :] = tail
        sib[e, pl.ds(lanes, 16), :] = tail


def core_sum_kernel(meta, own, recv, two_own, two_recv, p0, p1, p2, p3):
    rows = own.shape[1]
    for e, out in enumerate((p0, p1, p2, p3)):
        out[:rows, :] = (own[e] + recv[e]).astype(BF)
        x = lax.rem(meta[1] + e, NX)
        out[rows:, :] = (two_own[x] + two_recv[x].astype(F32)).astype(BF)


def four_sum(parts):
    p0, p1, p2, p3 = [p[...].astype(F32) for p in parts]
    return (p0 + p2) + (p1 + p3)


def x_sum_kernel(p0, p1, p2, p3, one, two):
    total = four_sum((p0, p1, p2, p3))
    rows = one.shape[0]
    one[...] = total[:rows].astype(BF)
    n = two.shape[1]
    for i in range(two.shape[0]):
        two[i] = total[rows + i * n : rows + (i + 1) * n]


def y_sum_kernel(p0, p1, p2, p3, grad, bias):
    total = four_sum((p0, p1, p2, p3))
    half = grad.shape[1]
    grad[0] = total[:half]
    grad[1] = total[half : 2 * half]
    bias[...] = total[2 * half : 2 * half + 1]


def all_to_all(value, axes):
    return lax.all_to_all(value, axes, split_axis=0, concat_axis=0, tiled=True)


def on_device(features, nbr_one, w_one, b_one, send_rows, nbr_slot, degree, w_two, cotangent):
    local = features[0]
    feats, group_nodes = local.shape
    fanout = nbr_one.shape[1]
    width = w_two.shape[1]
    owned = cotangent.shape[1]
    lanes = NC * feats
    per = CHIPS // STEPS
    core = lax.axis_index("core")
    x_at, y_at = lax.axis_index("x"), lax.axis_index("grp")
    meta = jnp.stack([core, x_at, y_at]).astype(jnp.int32)
    swap = lambda v: shift(v, "core", NC, 1)

    sibling = swap(local)
    w_all = lax.all_gather(w_one.reshape(-1, width), FEAT, axis=0, tiled=True)
    w_all = w_all.reshape(CHIPS * NC, 2, feats, width)

    deg_row = degree[0][None, :]
    cot = cotangent[0]
    slots = CHIPS * NC * NY * send_rows.shape[-1]
    d_table, d_self, counts = call(
        table_grad_kernel,
        (shape((slots, width), BF), shape((owned, width), F32), shape((slots, owned), BF)),
        [vmem()] * 4,
        (cot, w_two, nbr_slot, deg_row),
        "table_grad", us=3.0,
    )

    def exchange(rows):
        return all_to_all(rows.reshape(CHIPS * NC * NY, -1, width), ALL).reshape(-1, width)

    returned = exchange(d_table)

    by_device = nbr_one[0].reshape(fanout, CHIPS, NC, owned)
    idx = lax.dynamic_index_in_dim(by_device, core, 2, keepdims=False)
    idx = idx.transpose(1, 0, 2).reshape(-1)
    mean_shape = shape((CHIPS, owned, lanes), BF)
    mean_per = CHIPS // MEAN_STEPS
    acc = [pltpu.VMEM((owned, lanes), F32)]
    us_per = idx.shape[0] * 1e-3 / MEAN_STEPS
    table_shape = shape((group_nodes, lanes), F32)
    begun, mine, tbl = call(
        lambda *refs: first_mean_kernel(fanout, *refs),
        (mean_shape, mean_shape, table_shape),
        [smem(), smem(), whole(local.shape), whole(local.shape), unread()],
        (meta, idx, local, sibling, d_table),
        "mean_first", acc, us_per * FIRST_MEANS + 5.0, (FIRST_MEANS,),
        (
            pl.BlockSpec((mean_per, owned, lanes), lambda i: (i, 0, 0)),
            whole(mean_shape.shape), whole(table_shape.shape),
        ),
    )
    def over_x(value):
        by_x = value.reshape(NX, NZ, owned, lanes)
        pick = lambda d: lax.dynamic_index_in_dim(by_x, (x_at + d) % NX, 0, keepdims=False)
        return [shift(pick(d), "x", NX, d) if d else pick(0) for d in range(NX)]

    feats_here = all_to_all(mine, CHIP)
    lefts = over_x(mine)
    last = MEAN_STEPS - FIRST_MEANS
    means = call(
        lambda *refs: last_mean_kernel(fanout, *refs),
        mean_shape,
        [smem(), whole(tbl.shape), unread(), unread()],
        (idx, tbl, begun, returned),
        "mean_last", acc, us_per * last, (last,),
        pl.BlockSpec((mean_per, owned, lanes), lambda i: (i + FIRST_MEANS, 0, 0)),
        {2: 0},
    )
    means, *lefts = lax.optimization_barrier((means, *lefts))
    means_here = all_to_all(means, CHIP)

    left_spec = pl.BlockSpec((per, owned, lanes), lambda i: (i, 0, 0))

    def w_spec(part):
        return pl.BlockSpec((per * NC, 1, feats, width), lambda i: (i, part, 0, 0))

    self_part = call(
        self_kernel, shape((owned, width), F32), [left_spec, w_spec(0)], (feats_here, w_all),
        "self_part", us=4.0, grid=(STEPS,), out_specs=whole((owned, width)),
    )
    lefts = lefts + over_x(means)
    self_part, *lefts = lax.optimization_barrier((self_part, *lefts))

    send = send_rows[0, 0].reshape(1, -1)
    bias_row = b_one[None, :]
    ins = (self_part, bias_row, d_self, returned, send)
    outs = (shape((owned, width), BF), shape((owned, width), BF), shape((slots, width), BF))
    h_one, d_pre, outgoing = call(
        node_kernel,
        outs,
        [left_spec, w_spec(1)] + [whole(v.shape) for v in ins],
        (means_here, w_all, *ins),
        "node_update",
        [pltpu.VMEM((owned, width), F32)],
        us=4.0, grid=(STEPS,), out_specs=tuple(whole(o.shape) for o in outs),
    )
    d_pre_z = lax.all_gather(d_pre, "z", axis=0, tiled=True)
    table = exchange(outgoing)

    block_rows = 2 * width // (CHIPS * NC)
    emb, two_own, two_sib = call(
        layer_two_kernel,
        (
            shape((owned, width), BF),
            shape((CHIPS, block_rows, width), F32),
            shape((CHIPS, block_rows, width), BF),
        ),
        [smem()] + [vmem()] * 6,
        (meta, table, counts, deg_row, h_one, cot, w_two),
        "layer_two", us=3.0,
    )
    d_pre_z, two_sib = lax.optimization_barrier((d_pre_z, two_sib))
    two_recv = swap(two_sib)

    rows = 2 * feats + 16
    one_own, one_sib = call(
        weight_grad_kernel,
        (shape((NX, rows, width), F32), shape((NX, rows, width), F32)),
        [smem()] + [vmem()] * (2 * NX + 1),
        (meta, *lefts, d_pre_z),
        "weight_grad", us=15.0,
    )
    two_rows = NZ * block_rows
    sums = call(
        core_sum_kernel,
        (shape((rows + two_rows, width), BF),) * NX,
        [smem()] + [vmem()] * 4,
        (
            meta, one_own, swap(one_sib), two_own.reshape(NX, two_rows, width),
            two_recv.reshape(NX, two_rows, width),
        ),
        "core_sum", us=2.0,
    )
    got = [sums[0]] + [shift(sums[e], "x", NX, e) for e in range(1, NX)]
    total, two = call(
        x_sum_kernel, (shape((rows, width), BF), shape((NZ * NY, block_rows // NY, width), F32)),
        [vmem()] * NX,
        tuple(got), "x_sum",
    )
    grad_w_two = jnp.sum(all_to_all(two, ("z", "grp")), axis=0)
    got = [total] + [shift(total, "grp", NY, e) for e in range(1, NY)]
    grad_w_one, grad_b_one = call(
        y_sum_kernel,
        (shape((2, feats, width), F32), shape((1, width), F32)),
        [vmem()] * NY,
        tuple(got),
        "y_sum",
    )
    return emb[None], grad_w_one, grad_b_one[0], grad_w_two


def solution(mesh):
    parts = Mesh(mesh.devices.reshape(NX, NZ, NC, NY), ALL)
    return jax.shard_map(
        on_device,
        mesh=parts,
        in_specs=(
            P("grp", FEAT, None),
            P("grp", None, None),
            P(None, FEAT, None),
            P(),
            P("grp", FEAT, None, None, None),
            P("grp", None, FEAT),
            P("grp", FEAT),
            P(),
            P("grp", FEAT, None),
        ),
        out_specs=(P("grp", FEAT, None), P(None, FEAT, None), P(), P(ALL, None)),
        check_vma=False,
    )
```
